256 devices in a mesh: section: 8 (over y, x_lo), dev: 32 (over x_hi, z, core).
Axes of the slice: x: 4 (x_hi: 2, x_lo: 2; x = x_hi * 2 + x_lo), y: 4, z: 8, core: 2. Of those that a mesh axis runs over, the one named last changes fastest.
Arguments:
- acts: bfloat16 [2, 2048, 12288], P(None, None, ('section', 'dev')), may hold values from -45 to 45
- ln_gain: float32 [12288], P('section'), may hold values from 0.25 to 1.75
- ln_bias: float32 [12288], P('section'), may hold values from -3 to 3
- up_weight: bfloat16 [12288, 24576], P('section', 'dev'), may hold values from -0.0546875 to 0.0546875
- up_bias: float32 [24576], P('dev'), may hold values from -3 to 3
- down_weight: bfloat16 [24576, 6144], P('dev', 'section'), may hold values from -0.0390625 to 0.0390625
- down_bias: float32 [6144], P('section'), may hold values from -3 to 3
Outputs:
- layer_out: bfloat16 [2, 2048, 6144], P(None, 'dev', 'section')
The draws below stay inside these ranges and needn't reach their ends.
All inputs are finite; a program needn't handle non-finite values.
Results may differ from the reference program's by a relative error of at most 0.025.
Values may be sent and summed in bfloat16 or wider, within the bound.
No kernel may reach another device: no remote copies, remote signals or barrier semaphores. Data moves between devices by JAX's collectives and lax.ppermute only.
A program may use at most 64 MiB of HBM per device.

```python
import jax
import jax.numpy as jnp
from jax import lax

D = 12288
FFW = 24576
DOUT = 6144
MICRO = 2
SEQ = 2048
N_SECTION = 8
N_DEV = 32


def draw_acts(key, part):
    key = jax.random.fold_in(key, 11)
    key_values, key_rough, key_offsets = jax.random.split(key, 3)
    position = jnp.arange(D, dtype=jnp.float32) / D
    roughness = jnp.exp(jax.random.uniform(key_rough, (D,), jnp.float32, -0.5, 0.5))
    samples = jnp.clip(jax.random.normal(key_values, (MICRO, SEQ, D), jnp.float32), -6.0, 6.0)
    growth = 3.0 ** position
    offsets = 0.6 * position * jnp.exp(jax.random.uniform(key_offsets, (D,), jnp.float32, -0.5, 0.5))
    return (growth * roughness * (samples + offsets)).astype(jnp.bfloat16)


def levels(stream_key, dims, pieces, smallest, high):
    def one(dim, shards_of):
        steps = jax.random.uniform(jax.random.fold_in(jax.random.fold_in(stream_key, 6), dim), (shards_of,), jnp.float32, smallest / len(pieces), high / len(pieces))
        return jnp.repeat(jnp.exp(steps), dims[dim] // shards_of).reshape((-1,) + (1,) * (len(dims) - dim - 1))

    level = one(*pieces[0])
    for cut in pieces[1:]:
        level = level * one(*cut)
    return level


def scatter_about(key, shape, scale, most, cuts=(), kind=jnp.bfloat16):
    entries = jax.random.normal(key, shape, jnp.float32) * scale
    if len(cuts) > 0:
        entries = levels(key, shape, cuts, -0.22, 0.18) * entries
    return jnp.clip(entries, min=-most, max=most).astype(kind)


def setup_inputs(seed: int = 0) -> dict:
    key_of = jax.random.split(jax.random.key(seed), 8)
    acts = draw_acts(jax.random.fold_in(key_of[7], 71), 0)
    ln_gain = jnp.clip(1.0 + 0.15 * jax.random.normal(key_of[1], (D,), jnp.float32), 0.25, 1.75)
    ln_bias = scatter_about(key_of[2], (D,), 0.5, 3.0, ((0, 8),), jnp.float32)
    up_weight = scatter_about(key_of[3], (D, FFW), D ** -0.5, 0.0546875, ((0, 8), (1, 32)))
    up_bias = scatter_about(key_of[4], (FFW,), 0.5, 3.0, ((0, 32),), jnp.float32)
    down_weight = scatter_about(key_of[5], (FFW, DOUT), FFW ** -0.5, 0.0390625, ((0, 32), (1, 8)))
    down_bias = scatter_about(key_of[6], (DOUT,), 0.5, 3.0, ((0, 8),), jnp.float32)
    return {"acts": acts, "ln_gain": ln_gain, "ln_bias": ln_bias, "up_weight": up_weight, "up_bias": up_bias, "down_weight": down_weight, "down_bias": down_bias}


def block_sum(left, right, block_count):
    row_count, inner_len = left.shape
    block_len = inner_len // block_count
    left_blocks = jnp.transpose(left.reshape(row_count, block_count, block_len), (1, 0, 2))
    right_blocks = right.reshape(block_count, block_len, right.shape[1])

    def add_term(running, blocks):
        left_piece, weight = blocks
        rounded = lax.optimization_barrier(jnp.dot(left_piece, weight, preferred_element_type=jnp.float32).astype(jnp.bfloat16))
        return (running + rounded.astype(jnp.float32), None)
    running, unused = lax.scan(add_term, jnp.zeros((row_count, right.shape[1]), jnp.float32), (left_blocks, right_blocks))
    return running

def reference(acts, ln_gain, ln_bias, up_weight, up_bias, down_weight, down_bias):
    tokens = acts.reshape(MICRO * SEQ, D).astype(jnp.float32)
    center = lax.optimization_barrier(jnp.mean(tokens, axis=1, keepdims=True))
    deviation = tokens - center
    spread = lax.optimization_barrier(jnp.mean(deviation * deviation, axis=1, keepdims=True))
    normed = (deviation * lax.rsqrt(spread + 1e-05) * ln_gain + ln_bias).astype(jnp.bfloat16)
    up_total = block_sum(normed, up_weight, N_SECTION)
    hidden = jax.nn.gelu(up_total + up_bias, approximate=True).astype(jnp.bfloat16)
    out_total = block_sum(hidden, down_weight, N_DEV)
    return (out_total + down_bias).astype(jnp.bfloat16).reshape(MICRO, SEQ, DOUT)
```

```python
import jax
import jax.numpy as jnp
from jax import lax
from jax.sharding import Mesh, PartitionSpec as P

f32, bf16 = jnp.float32, jnp.bfloat16
NY, NXLO, NXHI, NZ, NCORE = 4, 2, 2, 8, 2
SEC = ("y", "xlo")
DEV = ("xhi", "z", "core")
NEAR = ("xlo", "xhi", "core")


def swap(x, axis):
    return lax.ppermute(x, axis, [(0, 1), (1, 0)])


def shift(x, d):
    return lax.ppermute(x, "y", [(i, (i + d) % NY) for i in range(NY)])


def near(x, mask):
    return lax.ppermute(x, NEAR, [(i, i ^ mask) for i in range(8)])


def ordered(which, own, other):
    first = which == 0
    return jnp.where(first, own, other), jnp.where(first, other, own)


def local(acts, ln_gain, ln_bias, w1, up_bias, w2, down_bias):
    micros, seq, width = acts.shape
    own_seq = seq // (NXHI * NZ * NCORE)
    chunk = NZ * own_seq
    tokens = NXHI * chunk
    y, xlo, xhi, core = (lax.axis_index(a) for a in ("y", "xlo", "xhi", "core"))
    features = width * 256

    tiles = acts.reshape(micros, NXHI, NZ, NCORE, own_seq, width)
    tiles = tiles.transpose(0, 3, 5, 1, 2, 4).reshape(micros, NCORE, width, tokens)
    mine, theirs = ordered(xlo, tiles[0], tiles[1])
    quarter = [ordered(core, part[0], part[1]) for part in (mine, theirs)]

    def arrived(rx, rh, rc):
        piece, mask = quarter[rx][rc], rx * 4 + rh * 2 + rc
        return near(piece, mask) if mask else piece

    rows = []
    for rx in range(2):
        by_hi = []
        for rh in range(2):
            a, b = ordered(core, arrived(rx, rh, 0), arrived(rx, rh, 1))
            by_hi.append(jnp.concatenate([a, b], axis=0))
        rows.append(jnp.stack(ordered(xhi, *by_hi)))
    x = jnp.stack(rows)

    x, w1 = lax.optimization_barrier((x, w1))
    w1s = [[w1, swap(w1, "core")]]
    far = swap(w1, "xlo")
    w1s.append([far, swap(far, "core")])
    far, w2 = lax.optimization_barrier((far, w2))
    far2 = swap(w2, "xlo")
    w2_cat = jnp.concatenate(
        [
            jnp.concatenate([w2, far2], axis=1),
            jnp.concatenate([swap(w2, "core"), swap(far2, "core")], axis=1),
        ],
        axis=0,
    )
    scale = jnp.stack([ln_gain, ln_bias])
    scale = jnp.stack([scale, swap(scale, "xlo")])
    scale = scale.reshape(NXLO, 2, NXHI, NZ, 2 * width).transpose(1, 3, 0, 2, 4)[..., None]
    biases = [up_bias, swap(up_bias, "core")]

    x32 = x.astype(f32)
    mean = lax.psum(jnp.sum(x32, axis=(0, 1, 2)), ("y", "z")) / features
    off = x32 - mean
    var = lax.psum(jnp.sum(off * off, axis=(0, 1, 2)), ("y", "z")) / features
    rstd = lax.rsqrt(var + 1e-05)

    outs = []
    for t in range(NXHI):
        cut = slice(t * chunk, (t + 1) * chunk)
        gathered = lax.all_gather(x[..., cut], "z")
        normed = (gathered.astype(f32) - mean[cut]) * rstd[cut] * scale[0] + scale[1]
        normed = normed.astype(bf16).transpose(1, 2, 0, 3, 4).reshape(NXLO, -1, chunk)
        part = chunk // NY
        hidden = jnp.zeros((chunk, NCORE * w1.shape[1]), bf16)
        for j in range(NCORE):
            up = sum(
                lax.dot_general(
                    normed[r], w1s[r][j], (((0,), (0,)), ((), ())), preferred_element_type=f32
                )
                for r in range(NXLO)
            ).astype(bf16)
            block = lambda d: lax.dynamic_slice_in_dim(up, (y + d) % NY * part, part, 0)
            total = block(0).astype(f32)
            for d in range(1, NY):
                total = total + shift(block(d), d).astype(f32)
            act = jax.nn.gelu(total + biases[j], approximate=True).astype(bf16)
            for d in range(NY):
                got = shift(act, d) if d else act
                hidden = lax.dynamic_update_slice(
                    hidden, got, ((y - d) % NY * part, j * w1.shape[1])
                )
        down = jnp.dot(hidden, w2_cat, preferred_element_type=f32).astype(bf16)
        outs.append(lax.psum_scatter(down, "z", scatter_dimension=0, tiled=True))

    keep, send = ordered(xhi, outs[0], outs[1])
    cols = down_bias.shape[0]
    here = keep[:, :cols].astype(f32) + near(send[:, :cols], 2).astype(f32)
    other = near(keep[:, cols:], 4).astype(f32) + near(send[:, cols:], 6).astype(f32)
    both = jnp.stack(ordered(xlo, here, other))
    return (both + down_bias).astype(bf16)


def solution(mesh):
    fine = Mesh(mesh.devices.reshape(NY, NXLO, NXHI, NZ, NCORE), SEC + DEV)
    in_specs = (
        P(None, None, SEC + DEV),
        P(SEC),
        P(SEC),
        P(SEC, DEV),
        P(DEV),
        P(DEV, SEC),
        P(SEC),
    )
    return jax.shard_map(
        local, mesh=fine, in_specs=in_specs, out_specs=P(None, DEV, SEC), check_vma=False
    )
```

```python
import jax
import jax.numpy as jnp
from jax import lax
from jax.sharding import Mesh, PartitionSpec as P

f32, bf16 = jnp.float32, jnp.bfloat16
NY, NXLO, NXHI, NZ, NCORE = 4, 2, 2, 8, 2
SEC = ("y", "xlo")
DEV = ("xhi", "z", "core")
NEAR = ("xlo", "xhi", "core")


def swap(x, axis):
    return lax.ppermute(x, axis, [(0, 1), (1, 0)])


def shift(x, axis, d):
    n = lax.axis_size(axis)
    return lax.ppermute(x, axis, [(i, (i + d) % n) for i in range(n)])


def near(x, mask):
    return lax.ppermute(x, NEAR, [(i, i ^ mask) for i in range(8)])


def ordered(which, own, other):
    first = which == 0
    return jnp.where(first, own, other), jnp.where(first, other, own)


def ring_sum(down, z):
    rows, cols = down.shape[0] // NZ, down.shape[1]
    half = cols // 2

    def block(d):
        return lax.dynamic_slice_in_dim(down, (z + d) % NZ * rows, rows, 0)

    def add(a, b):
        return (a.astype(f32) + b.astype(f32)).astype(bf16)

    opposite = block(NZ // 2)
    up = shift(opposite[:, :half], "z", 1)
    dn = shift(opposite[:, half:], "z", -1)
    for d in range(NZ // 2 - 1, 0, -1):
        a, b = block(d), block(-d)
        if d == NZ // 2 - 1:
            a = jnp.concatenate([add(a[:, :half], up), a[:, half:]], axis=1)
            b = jnp.concatenate([b[:, :half], add(b[:, half:], dn)], axis=1)
        else:
            a, b = add(a, up), add(b, dn)
        up, dn = shift(a, "z", 1), shift(b, "z", -1)
    return block(0).astype(f32) + up.astype(f32) + dn.astype(f32)


def local(acts, ln_gain, ln_bias, w1, up_bias, w2, down_bias):
    micros, seq, width = acts.shape
    own_seq = seq // (NXHI * NZ * NCORE)
    chunk = NZ * own_seq
    tokens = NXHI * chunk
    y, xlo, xhi, z, core = (lax.axis_index(a) for a in ("y", "xlo", "xhi", "z", "core"))
    features = width * 256
    group = features // NY

    tiles = acts.reshape(micros, NXHI, NZ, NCORE, own_seq, width)
    tiles = tiles.transpose(0, 3, 5, 1, 2, 4).reshape(micros, NCORE, width, tokens)
    mine, theirs = ordered(xlo, tiles[0], tiles[1])
    quarter = [ordered(core, part[0], part[1]) for part in (mine, theirs)]

    def arrived(rx, rh, rc):
        piece, mask = quarter[rx][rc], rx * 4 + rh * 2 + rc
        return near(piece, mask) if mask else piece

    rows = []
    for rx in range(2):
        by_hi = []
        for rh in range(2):
            a, b = ordered(core, arrived(rx, rh, 0), arrived(rx, rh, 1))
            by_hi.append(jnp.concatenate([a, b], axis=0))
        rows.append(jnp.stack(ordered(xhi, *by_hi)))
    x = jnp.stack(rows)

    k1, n1 = w1.shape
    scaled = (w1.astype(f32) * ln_gain[:, None]).astype(bf16)
    col = jnp.sum(scaled.astype(f32), axis=0)
    shiftv = jnp.sum(w1.astype(f32) * ln_bias[:, None], axis=0)
    vec = jnp.stack([col, shiftv])
    vec = vec + swap(vec, "xlo")
    vec = jnp.stack([vec, swap(vec, "core")])
    vecs = [vec] + [shift(vec, "y", d) for d in range(1, NY)]
    offset = sum(v[:, 1] for v in vecs) + jnp.stack([up_bias, swap(up_bias, "core")])

    scaled = scaled.reshape(NXHI, NZ, 2 * width, n1).transpose(1, 0, 2, 3).reshape(k1, n1)
    x, vec, scaled = lax.optimization_barrier((x, vec, scaled))
    w1s = [[scaled, swap(scaled, "core")]]
    far = swap(scaled, "xlo")
    w1s.append([far, swap(far, "core")])
    far, w2 = lax.optimization_barrier((far, w2))
    far2 = swap(w2, "xlo")
    w2_cat = jnp.concatenate(
        [
            jnp.concatenate([w2, far2], axis=1),
            jnp.concatenate([swap(w2, "core"), swap(far2, "core")], axis=1),
        ],
        axis=0,
    )

    outs = []
    for t in range(NXHI):
        gathered = lax.all_gather(x[..., t * chunk : (t + 1) * chunk], "z")
        part = chunk // NY
        g32 = gathered.astype(f32)
        mean = jnp.sum(g32, axis=(0, 1, 2, 3)) / group
        dev = g32 - mean
        stats = jnp.stack([mean, jnp.sum(dev * dev, axis=(0, 1, 2, 3))])
        ups = []
        for j in range(NCORE):
            acc = sum(
                lax.dot_general(
                    gathered[:, r].reshape(k1, chunk),
                    w1s[r][j],
                    (((0,), (0,)), ((), ())),
                    preferred_element_type=f32,
                )
                for r in range(NXLO)
            )
            ups.append((acc - mean[:, None] * vec[j, 0][None, :]).astype(bf16))

        def block(d):
            at = (y + d) % NY * part
            return jnp.concatenate(
                [lax.dynamic_slice_in_dim(up, at, part, 0) for up in ups], axis=1
            )

        def own_stats(d):
            return lax.dynamic_slice_in_dim(stats, (y + d) % NY * part, part, 1)

        total = block(0).astype(f32)
        for d in (2, 1, 3):
            total = total + shift(block(d), "y", d).astype(f32)
        every = [own_stats(0)] + [shift(own_stats(d), "y", d) for d in range(1, NY)]
        center = sum(s[0] for s in every) / NY
        spread = sum(s[1] + group * jnp.square(s[0] - center) for s in every) / features
        for s, v in zip(every, vecs):
            total = total + (s[0] - center)[:, None] * v[:, 0].reshape(1, -1)
        total = total * lax.rsqrt(spread + 1e-05)[:, None] + offset.reshape(1, -1)
        act = jax.nn.gelu(total, approximate=True).astype(bf16)
        hidden = jnp.zeros((chunk, NCORE * n1), bf16)
        for d in range(NY):
            got = shift(act, "y", d) if d else act
            hidden = lax.dynamic_update_slice_in_dim(hidden, got, (y - d) % NY * part, 0)
        down = jnp.dot(hidden, w2_cat, preferred_element_type=f32).astype(bf16)
        outs.append(ring_sum(down, z).astype(bf16))

    keep, send = ordered(xhi, outs[0], outs[1])
    cols = down_bias.shape[0]
    here = keep[:, :cols].astype(f32) + near(send[:, :cols], 2).astype(f32)
    other = near(keep[:, cols:], 4).astype(f32) + near(send[:, cols:], 6).astype(f32)
    both = jnp.stack(ordered(xlo, here, other))
    return (both + down_bias).astype(bf16)


def solution(mesh):
    fine = Mesh(mesh.devices.reshape(NY, NXLO, NXHI, NZ, NCORE), SEC + DEV)
    in_specs = (
        P(None, None, SEC + DEV),
        P(SEC),
        P(SEC),
        P(SEC, DEV),
        P(DEV),
        P(DEV, SEC),
        P(SEC),
    )
    return jax.shard_map(
        local, mesh=fine, in_specs=in_specs, out_specs=P(None, DEV, SEC), check_vma=False
    )
```

```python
import jax
import jax.numpy as jnp
from jax import lax
from jax.sharding import Mesh, PartitionSpec as P

f32, bf16 = jnp.float32, jnp.bfloat16
NY, NXLO, NXHI, NZ, NCORE = 4, 2, 2, 8, 2
SEC = ("y", "xlo")
DEV = ("xhi", "z", "core")
NEAR = ("xlo", "xhi", "core")


def swap(x, axis):
    return lax.ppermute(x, axis, [(0, 1), (1, 0)])


def shift(x, axis, d):
    n = lax.axis_size(axis)
    return lax.ppermute(x, axis, [(i, (i + d) % n) for i in range(n)])


def near(x, mask):
    return lax.ppermute(x, NEAR, [(i, i ^ mask) for i in range(8)])


def flip(x, axis, bit):
    return lax.ppermute(x, axis, [(i, i ^ bit) for i in range(lax.axis_size(axis))])


def after(x, other):
    return lax.optimization_barrier((x, other))[0]


def ordered(which, own, other):
    first = which == 0
    return jnp.where(first, own, other), jnp.where(first, other, own)


def ring_sum(down, z):
    rows, cols = down.shape[0] // NZ, down.shape[1]
    half = cols // 2

    def block(d):
        return lax.dynamic_slice_in_dim(down, (z + d) % NZ * rows, rows, 0)

    def add(a, b):
        return (a.astype(f32) + b.astype(f32)).astype(bf16)

    opposite = block(NZ // 2)
    up = shift(opposite[:, :half], "z", 1)
    dn = shift(opposite[:, half:], "z", -1)
    for d in range(NZ // 2 - 1, 0, -1):
        a, b = block(d), block(-d)
        if d == NZ // 2 - 1:
            a = jnp.concatenate([add(a[:, :half], up), a[:, half:]], axis=1)
            b = jnp.concatenate([b[:, :half], add(b[:, half:], dn)], axis=1)
        else:
            a, b = add(a, up), add(b, dn)
        up, dn = shift(a, "z", 1), shift(b, "z", -1)
    return block(0).astype(f32) + up.astype(f32) + dn.astype(f32)


def local(acts, ln_gain, ln_bias, w1, up_bias, w2, down_bias):
    micros, seq, width = acts.shape
    own_seq = seq // (NXHI * NZ * NCORE)
    chunk = NZ * own_seq
    tokens = NXHI * chunk
    y, xlo, xhi, z, core = (lax.axis_index(a) for a in ("y", "xlo", "xhi", "z", "core"))
    features = width * 256

    tiles = acts.reshape(micros, NXHI, NZ, NCORE, own_seq, width)
    tiles = tiles.transpose(0, 3, 5, 1, 2, 4).reshape(micros, NCORE, width, tokens)
    mine, theirs = ordered(xlo, tiles[0], tiles[1])
    quarter = [ordered(core, part[0], part[1]) for part in (mine, theirs)]

    def arrived(rx, rh, rc):
        piece, mask = quarter[rx][rc], rx * 4 + rh * 2 + rc
        return near(piece, mask) if mask else piece

    pieces = [[[arrived(rx, rh, rc) for rc in range(2)] for rh in range(2)] for rx in range(2)]
    rows = []
    for rx in range(2):
        by_hi = []
        for rh in range(2):
            a, b = ordered(core, *pieces[rx][rh])
            by_hi.append(jnp.concatenate([a, b], axis=0))
        rows.append(jnp.stack(ordered(xhi, *by_hi)))
    x = jnp.stack(rows)

    k1, n1 = w1.shape
    w1 = after(w1, pieces[0][0][1])
    scaled = (w1.astype(f32) * ln_gain[:, None]).astype(bf16)
    col = jnp.sum(scaled.astype(f32), axis=0)
    add = jnp.sum(w1.astype(f32) * ln_bias[:, None], axis=0)
    vec = jnp.stack([col, add])
    vec = vec + swap(vec, "xlo")
    vec = jnp.stack([vec, swap(vec, "core")])
    bias = jnp.concatenate([up_bias, swap(up_bias, "core")])

    scaled = scaled.reshape(NXHI, NZ, 2 * width, n1).transpose(1, 0, 2, 3).reshape(k1, n1)
    x, scaled = lax.optimization_barrier((x, scaled))
    w1s = [[scaled, swap(scaled, "core")]]
    far = swap(scaled, "xlo")
    w1s.append([far, swap(far, "core")])
    far2 = swap(after(w2, far), "xlo")
    w2_cat = jnp.concatenate(
        [
            jnp.concatenate([w2, far2], axis=1),
            jnp.concatenate([swap(w2, "core"), swap(far2, "core")], axis=1),
        ],
        axis=0,
    )

    count = x.shape[0] * x.shape[1] * x.shape[2]
    x32 = x.astype(f32)
    mean = jnp.sum(x32, axis=(0, 1, 2)) / count
    m2 = jnp.sum(jnp.square(x32 - mean), axis=(0, 1, 2))
    for axis, bit in (("y", 1), ("y", 2), ("z", 1), ("z", 2), ("z", 4)):
        theirs = flip(jnp.stack([mean, m2]), axis, bit)
        m2 = m2 + theirs[1] + (count / 2) * jnp.square(mean - theirs[0])
        mean = (mean + theirs[0]) / 2
        count = 2 * count
    rstd = lax.rsqrt(m2 / features + 1e-05)

    part = chunk // NY

    def project_up(t, gathered):
        cut = slice(t * chunk, (t + 1) * chunk)
        ups = []
        for j in range(NCORE):
            acc = sum(
                lax.dot_general(
                    gathered[:, r].reshape(k1, chunk),
                    w1s[r][j],
                    (((0,), (0,)), ((), ())),
                    preferred_element_type=f32,
                )
                for r in range(NXLO)
            )
            up = (acc - mean[cut, None] * vec[j, 0]) * rstd[cut, None] + vec[j, 1]
            ups.append(up.astype(bf16))
        return ups

    def spread(ups):
        def block(d):
            at = (y + d) % NY * part
            return jnp.concatenate(
                [lax.dynamic_slice_in_dim(up, at, part, 0) for up in ups], axis=1
            )

        return [block(0)] + [shift(block(d), "y", d) for d in (2, 1, 3)]

    def activate(terms):
        total = sum(term.astype(f32) for term in terms)
        return jax.nn.gelu(total + bias, approximate=True).astype(bf16)

    def share(act):
        return [act] + [shift(act, "y", d) for d in range(1, NY)]

    def project_down(acts):
        hidden = jnp.zeros((chunk, NCORE * n1), bf16)
        for d in range(NY):
            hidden = lax.dynamic_update_slice_in_dim(hidden, acts[d], (y - d) % NY * part, 0)
        return jnp.dot(hidden, w2_cat, preferred_element_type=f32).astype(bf16)

    gathers = [lax.all_gather(x[..., t * chunk : (t + 1) * chunk], "z") for t in range(NXHI)]
    up0 = project_up(0, gathers[0])
    act0 = activate(spread(up0))
    acts0 = share(act0)
    up1 = project_up(1, after(gathers[1], act0))
    down0 = project_down([act0] + after(acts0[1:], up1))
    outs = [lax.psum_scatter(down0, "z", scatter_dimension=0, tiled=True)]
    terms1 = spread(up1)
    act1 = activate(terms1[:1] + after(terms1[1:], down0))
    acts1 = share(act1)
    down1 = project_down([act1] + after(acts1[1:], outs[0]))
    outs.append(ring_sum(down1, z).astype(bf16))

    keep, send = ordered(xhi, outs[0], outs[1])
    cols = down_bias.shape[0]
    here = keep[:, :cols].astype(f32) + near(send[:, :cols], 2).astype(f32)
    other = near(keep[:, cols:], 4).astype(f32) + near(send[:, cols:], 6).astype(f32)
    both = jnp.stack(ordered(xlo, here, other))
    return (both + down_bias).astype(bf16)


def solution(mesh):
    fine = Mesh(mesh.devices.reshape(NY, NXLO, NXHI, NZ, NCORE), SEC + DEV)
    in_specs = (
        P(None, None, SEC + DEV),
        P(SEC),
        P(SEC),
        P(SEC, DEV),
        P(DEV),
        P(DEV, SEC),
        P(SEC),
    )
    return jax.shard_map(
        local, mesh=fine, in_specs=in_specs, out_specs=P(None, DEV, SEC), check_vma=False
    )
```

```python
import jax
import jax.numpy as jnp
from jax import lax
from jax.sharding import Mesh, PartitionSpec as P

f32, bf16 = jnp.float32, jnp.bfloat16
NY, NXLO, NXHI, NZ, NCORE = 4, 2, 2, 8, 2
SEC = ("y", "xlo")
DEV = ("xhi", "z", "core")
NEAR = ("xlo", "xhi", "core")


def swap(x, axis):
    return lax.ppermute(x, axis, [(0, 1), (1, 0)])


def turn(x, axis, d):
    n = lax.axis_size(axis)
    pairs = [(i * 2 + c, (i + d * (1 - 2 * c)) % n * 2 + c) for i in range(n) for c in range(2)]
    return lax.ppermute(x, (axis, "core"), pairs)


def near(x, mask):
    return lax.ppermute(x, NEAR, [(i, i ^ mask) for i in range(8)])


def flip(x, axis, bit):
    return lax.ppermute(x, axis, [(i, i ^ bit) for i in range(lax.axis_size(axis))])


def after(x, other):
    return lax.optimization_barrier((x, other))[0]


def ordered(which, own, other):
    first = which == 0
    return jnp.where(first, own, other), jnp.where(first, other, own)


def add(a, b):
    return (a.astype(f32) + b.astype(f32)).astype(bf16)


def ring_sum(down, z, way):
    rows, cols = down.shape[0] // NZ, down.shape[1]
    half = cols // 2

    def block(d):
        return lax.dynamic_slice_in_dim(down, (z + d * way + NZ) % NZ * rows, rows, 0)

    opposite = block(NZ // 2)
    there = turn(opposite[:, :half], "z", 1)
    back = turn(opposite[:, half:], "z", -1)
    for d in range(NZ // 2 - 1, 0, -1):
        a, b = block(d), block(-d)
        if d == NZ // 2 - 1:
            a = jnp.concatenate([add(a[:, :half], there), a[:, half:]], axis=1)
            b = jnp.concatenate([b[:, :half], add(b[:, half:], back)], axis=1)
        else:
            a, b = add(a, there), add(b, back)
        there, back = turn(a, "z", 1), turn(b, "z", -1)
    return block(0).astype(f32) + there.astype(f32) + back.astype(f32)


def ring_gather(x, z, way):
    whole = [jnp.zeros((NZ,) + x.shape[1:], x.dtype) for _ in range(2)]
    for d in range(NZ):
        x = turn(x, "z", 1) if d else x
        source = (z - d * way + NZ) % NZ
        whole = [lax.dynamic_update_slice_in_dim(w, x[r : r + 1], source, 0) for r, w in enumerate(whole)]
    return whole


def local(acts, ln_gain, ln_bias, w1, up_bias, w2, down_bias):
    micros, seq, width = acts.shape
    own_seq = seq // (NXHI * NZ * NCORE)
    chunk = NZ * own_seq
    tokens = NXHI * chunk
    y, xlo, xhi, z, core = (lax.axis_index(a) for a in ("y", "xlo", "xhi", "z", "core"))
    features = width * 256
    way = 1 - 2 * core

    tiles = acts.reshape(micros, NXHI, NZ, NCORE, own_seq, width)
    tiles = tiles.transpose(0, 3, 5, 1, 2, 4).reshape(micros, NCORE, width, tokens)
    mine, theirs = ordered(xlo, tiles[0], tiles[1])
    quarter = [ordered(core, part[0], part[1]) for part in (mine, theirs)]

    def arrived(rx, rh, rc):
        piece, mask = quarter[rx][rc], rx * 4 + rh * 2 + rc
        return near(piece, mask) if mask else piece

    pieces = [[[arrived(rx, rh, rc) for rc in range(2)] for rh in range(2)] for rx in range(2)]
    rows = []
    for rx in range(2):
        by_hi = []
        for rh in range(2):
            a, b = ordered(core, *pieces[rx][rh])
            by_hi.append(jnp.concatenate([a, b], axis=0))
        rows.append(jnp.stack(ordered(xhi, *by_hi)))
    x = jnp.stack(rows)

    k1, n1 = w1.shape
    w1 = after(w1, pieces[0][0][1])
    scaled = (w1.astype(f32) * ln_gain[:, None]).astype(bf16)
    col = jnp.sum(scaled.astype(f32), axis=0)
    shifted = jnp.sum(w1.astype(f32) * ln_bias[:, None], axis=0)
    vec = jnp.stack([col, shifted])
    vec = vec + swap(vec, "xlo")
    scaled = after(scaled, vec)
    vec = jnp.stack([vec, swap(vec, "core")])
    bias = jnp.concatenate([up_bias, swap(up_bias, "core")])

    scaled = scaled.reshape(NXHI, NZ, 2 * width, n1).transpose(1, 0, 2, 3).reshape(k1, n1)
    x, scaled = lax.optimization_barrier((x, scaled))
    w1s = [[scaled, swap(scaled, "core")]]
    far = swap(scaled, "xlo")
    w1s.append([far, swap(far, "core")])
    far2 = swap(after(w2, far), "xlo")
    w2_cat = jnp.concatenate(
        [
            jnp.concatenate([w2, far2], axis=1),
            jnp.concatenate([swap(w2, "core"), swap(far2, "core")], axis=1),
        ],
        axis=0,
    )

    part = chunk // NY

    def statistics(gathered):
        count = NXLO * k1
        mean = sum(jnp.sum(g, axis=(0, 1), dtype=f32) for g in gathered) / count
        m2 = sum(jnp.sum(jnp.square(g.astype(f32) - mean), axis=(0, 1)) for g in gathered)
        for bit in (1, 2):
            theirs = flip(jnp.stack([mean, m2]), "y", bit)
            m2 = m2 + theirs[1] + (count / 2) * jnp.square(mean - theirs[0])
            mean = (mean + theirs[0]) / 2
            count = 2 * count
        return mean[:, None], lax.rsqrt(m2 / features + 1e-05)[:, None]

    def project_up(gathered, mean, rstd):
        ups = []
        for j in range(NCORE):
            acc = sum(
                lax.dot_general(
                    gathered[r].reshape(k1, chunk),
                    w1s[r][j],
                    (((0,), (0,)), ((), ())),
                    preferred_element_type=f32,
                )
                for r in range(NXLO)
            )
            ups.append(((acc - mean * vec[j, 0]) * rstd + vec[j, 1]).astype(bf16))
        return ups

    def spread(ups):
        def block(d):
            at = (y + d + NY) % NY * part
            return jnp.concatenate(
                [lax.dynamic_slice_in_dim(up, at, part, 0) for up in ups], axis=1
            )

        opposite = turn(block(2), "y", 1)
        near_by = turn(block(-way), "y", -1)
        return [block(0), near_by, turn(add(block(way), opposite), "y", 1)]

    def activate(terms):
        total = sum(term.astype(f32) for term in terms)
        return jax.nn.gelu(total + bias, approximate=True).astype(bf16)

    def share(act):
        first = turn(act, "y", 1)
        return [first, turn(act, "y", -1), turn(first, "y", 1)]

    def project_down(act, others):
        hidden = jnp.zeros((chunk, NCORE * n1), bf16)
        for d, got in zip((0, -way, way, 2), [act] + others):
            hidden = lax.dynamic_update_slice_in_dim(hidden, got, (y + d + NY) % NY * part, 0)
        return jnp.dot(hidden, w2_cat, preferred_element_type=f32).astype(bf16)

    flat = x.reshape(NXLO, NXHI * 2 * width, tokens)
    gathers = [ring_gather(flat[..., t * chunk : (t + 1) * chunk], z, way) for t in range(NXHI)]
    stats = [statistics(g) for g in gathers]
    up0 = project_up(gathers[0], *stats[0])
    act0 = activate(spread(up0))
    acts0 = share(act0)
    up1 = project_up(after(gathers[1], acts0[0]), *stats[1])
    down0 = project_down(act0, after(acts0, up1))
    outs = [lax.psum_scatter(down0, "z", scatter_dimension=0, tiled=True)]
    terms1 = spread(up1)
    act1 = activate(terms1[:1] + after(terms1[1:], down0))
    down1 = project_down(act1, after(share(act1), outs[0]))
    outs.append(ring_sum(down1, z, way).astype(bf16))

    keep, send = ordered(xhi, outs[0], outs[1])
    cols = down_bias.shape[0]
    here = keep[:, :cols].astype(f32) + near(send[:, :cols], 2).astype(f32)
    other = near(keep[:, cols:], 4).astype(f32) + near(send[:, cols:], 6).astype(f32)
    both = jnp.stack(ordered(xlo, here, other))
    return (both + down_bias).astype(bf16)


def solution(mesh):
    fine = Mesh(mesh.devices.reshape(NY, NXLO, NXHI, NZ, NCORE), SEC + DEV)
    in_specs = (
        P(None, None, SEC + DEV),
        P(SEC),
        P(SEC),
        P(SEC, DEV),
        P(DEV),
        P(DEV, SEC),
        P(SEC),
    )
    return jax.shard_map(
        local, mesh=fine, in_specs=in_specs, out_specs=P(None, DEV, SEC), check_vma=False
    )
```

```python
import jax
import jax.numpy as jnp
from jax import lax
from jax.sharding import Mesh, PartitionSpec as P

f32, bf16 = jnp.float32, jnp.bfloat16
NY, NXLO, NXHI, NZ, NCORE = 4, 2, 2, 8, 2
SEC = ("y", "xlo")
DEV = ("xhi", "z", "core")
NEAR = ("xlo", "xhi", "core")


def swap(x, axis):
    return lax.ppermute(x, axis, [(0, 1), (1, 0)])


def turn(x, axis, d):
    n = lax.axis_size(axis)
    pairs = [(i * 2 + c, (i + d * (1 - 2 * c)) % n * 2 + c) for i in range(n) for c in range(2)]
    return lax.ppermute(x, (axis, "core"), pairs)


def near(x, mask):
    return lax.ppermute(x, NEAR, [(i, i ^ mask) for i in range(8)])


def flip(x, axis, bit):
    return lax.ppermute(x, axis, [(i, i ^ bit) for i in range(lax.axis_size(axis))])


def after(x, other):
    return lax.optimization_barrier((x, other))[0]


def ordered(which, own, other):
    first = which == 0
    return jnp.where(first, own, other), jnp.where(first, other, own)


def add(a, b):
    return (a.astype(f32) + b.astype(f32)).astype(bf16)


def ring_sum(down, z, way):
    rows, cols = down.shape[0] // NZ, down.shape[1]
    half = cols // 2

    def block(d):
        return lax.dynamic_slice_in_dim(down, (z + d * way + NZ) % NZ * rows, rows, 0)

    opposite = block(NZ // 2)
    there = turn(opposite[:, :half], "z", 1)
    back = turn(opposite[:, half:], "z", -1)
    for d in range(NZ // 2 - 1, 0, -1):
        a, b = block(d), block(-d)
        if d == NZ // 2 - 1:
            a = jnp.concatenate([add(a[:, :half], there), a[:, half:]], axis=1)
            b = jnp.concatenate([b[:, :half], add(b[:, half:], back)], axis=1)
        else:
            a, b = add(a, there), add(b, back)
        there, back = turn(a, "z", 1), turn(b, "z", -1)
    return block(0).astype(f32) + there.astype(f32) + back.astype(f32)


def ring_gather(first, second, z, way):
    moving = [first, second]
    whole = [[jnp.zeros((NZ,) + m.shape[1:], m.dtype) for _ in range(2)] for m in moving]
    for d in range(NZ):
        if d == 1:
            moving[0] = arrival = turn(moving[0], "z", 1)
            moving[1] = turn(after(moving[1], arrival), "z", 1)
        elif d:
            moving = [turn(m, "z", 1) for m in moving]
        source = (z - d * way + NZ) % NZ
        whole = [
            [lax.dynamic_update_slice_in_dim(w, m[r : r + 1], source, 0) for r, w in enumerate(pair)]
            for pair, m in zip(whole, moving)
        ]
    return whole, arrival


def local(acts, ln_gain, ln_bias, w1, up_bias, w2, down_bias):
    micros, seq, width = acts.shape
    own_seq = seq // (NXHI * NZ * NCORE)
    chunk = NZ * own_seq
    tokens = NXHI * chunk
    y, xlo, xhi, z, core = (lax.axis_index(a) for a in ("y", "xlo", "xhi", "z", "core"))
    features = width * 256
    way = 1 - 2 * core

    tiles = acts.reshape(micros, NXHI, NZ, NCORE, own_seq, width)
    tiles = tiles.transpose(0, 3, 5, 1, 2, 4).reshape(micros, NCORE, width, tokens)
    mine, theirs = ordered(xlo, tiles[0], tiles[1])
    quarter = [ordered(core, part[0], part[1]) for part in (mine, theirs)]

    def arrived(rx, rh, rc):
        piece, mask = quarter[rx][rc], rx * 4 + rh * 2 + rc
        return near(piece, mask) if mask else piece

    pieces = [[[arrived(rx, rh, rc) for rc in range(2)] for rh in range(2)] for rx in range(2)]
    rows = []
    for rx in range(2):
        by_hi = []
        for rh in range(2):
            a, b = ordered(core, *pieces[rx][rh])
            by_hi.append(jnp.concatenate([a, b], axis=0))
        rows.append(jnp.stack(ordered(xhi, *by_hi)))
    x = jnp.stack(rows)

    flat = x.reshape(NXLO, NXHI * 2 * width, tokens)
    gathers, arrival = ring_gather(flat[..., :chunk], flat[..., chunk:], z, way)

    k1, n1 = w1.shape
    w1 = after(w1, pieces[0][0][1])
    scaled = (w1.astype(f32) * ln_gain[:, None]).astype(bf16)
    col = jnp.sum(scaled.astype(f32), axis=0)
    shifted = jnp.sum(w1.astype(f32) * ln_bias[:, None], axis=0)
    vec = jnp.stack([col, shifted])
    vec = vec + swap(vec, "xlo")
    scaled = after(scaled, vec)
    vec = after(vec, arrival)
    vec = jnp.stack([vec, swap(vec, "core")])

    scaled = scaled.reshape(NXHI, NZ, 2 * width, n1).transpose(1, 0, 2, 3).reshape(k1, n1)
    scaled = after(scaled, x)
    w1s = [[scaled, swap(scaled, "core")]]
    far = swap(scaled, "xlo")
    w1s.append([far, swap(far, "core")])
    far2 = swap(after(w2, far), "xlo")

    part = chunk // NY

    def join(axis, bits, count, mean, m2, extra):
        for bit in bits:
            n = mean.shape[0]
            theirs = flip(jnp.concatenate([mean, m2, extra]), axis, bit)
            their_mean, their_m2 = theirs[:n], theirs[n : 2 * n]
            m2 = m2 + their_m2 + (count / 2) * jnp.square(mean - their_mean)
            mean = (mean + their_mean) / 2
            extra = extra + theirs[2 * n :]
            count = 2 * count
        return count, mean, m2, extra

    count = x.shape[0] * x.shape[1] * x.shape[2]
    x32 = after(x, arrival).astype(f32)
    mean = jnp.sum(x32, axis=(0, 1, 2)) / count
    m2 = jnp.sum(jnp.square(x32 - mean), axis=(0, 1, 2))
    count, pivot, m2, total_vec = join("y", (1, 2), count, mean, m2, vec.reshape(-1))
    total_vec = total_vec.reshape(vec.shape)
    total_col = total_vec[:, 0].reshape(-1)
    bias = total_vec[:, 1].reshape(-1) + jnp.concatenate([up_bias, swap(up_bias, "core")])

    def project_up(t, gathered):
        mean = pivot[t * chunk : (t + 1) * chunk, None]
        ups = []
        for j in range(NCORE):
            acc = sum(
                lax.dot_general(
                    gathered[r].reshape(k1, chunk),
                    w1s[r][j],
                    (((0,), (0,)), ((), ())),
                    preferred_element_type=f32,
                )
                for r in range(NXLO)
            )
            ups.append((acc - mean * vec[j, 0]).astype(bf16))
        return ups

    def spread(ups):
        def block(d):
            at = (y + d + NY) % NY * part
            return jnp.concatenate(
                [lax.dynamic_slice_in_dim(up, at, part, 0) for up in ups], axis=1
            )

        opposite = turn(block(2), "y", 1)
        near_by = turn(block(-way), "y", -1)
        return [block(0), near_by, turn(add(block(way), opposite), "y", 1)], opposite

    def activate(t, terms):
        total = sum(term.astype(f32) for term in terms)
        rows = [lax.dynamic_slice_in_dim(v, t * chunk + y * part, part)[:, None] for v in (moved, rstd)]
        total = (total + rows[0] * total_col) * rows[1] + bias
        return jax.nn.gelu(total, approximate=True).astype(bf16)

    def share(act):
        first = turn(act, "y", 1)
        return [first, turn(act, "y", -1), turn(first, "y", 1)]

    def project_down(w2_cat, act, others):
        hidden = jnp.zeros((chunk, NCORE * n1), bf16)
        for d, got in zip((0, -way, way, 2), [act] + others):
            hidden = lax.dynamic_update_slice_in_dim(hidden, got, (y + d + NY) % NY * part, 0)
        return jnp.dot(hidden, w2_cat, preferred_element_type=f32).astype(bf16)

    pivot_z, m2_z = after((pivot, m2), gathers[1])
    _, mean, m2, _ = join("z", (1, 2, 4), count, pivot_z, m2_z, pivot_z[:0])
    rstd = lax.rsqrt(m2 / features + 1e-05)
    moved = pivot - mean

    up0 = project_up(0, gathers[0])
    terms0, opposite0 = spread(up0)
    up1 = project_up(1, after(gathers[1], up0))
    terms1, _ = spread(after(up1, opposite0))
    act0 = activate(0, after(terms0, up1))
    acts0 = share(act0)
    far2 = after(far2, act0)
    w2_cat = jnp.concatenate(
        [
            jnp.concatenate([w2, far2], axis=1),
            jnp.concatenate([swap(w2, "core"), swap(far2, "core")], axis=1),
        ],
        axis=0,
    )
    act1 = activate(1, after(terms1, act0))
    acts1 = share(act1)
    down0 = project_down(w2_cat, act0, after(acts0, act1))
    outs = [lax.psum_scatter(down0, "z", scatter_dimension=0, tiled=True)]
    down1 = project_down(w2_cat, act1, after(acts1, down0))
    outs.append(ring_sum(down1, z, way).astype(bf16))

    keep, send = ordered(xhi, outs[0], outs[1])
    cols = down_bias.shape[0]
    here = keep[:, :cols].astype(f32) + near(send[:, :cols], 2).astype(f32)
    other = near(keep[:, cols:], 4).astype(f32) + near(send[:, cols:], 6).astype(f32)
    both = jnp.stack(ordered(xlo, here, other))
    return (both + down_bias).astype(bf16)


def solution(mesh):
    fine = Mesh(mesh.devices.reshape(NY, NXLO, NXHI, NZ, NCORE), SEC + DEV)
    in_specs = (
        P(None, None, SEC + DEV),
        P(SEC),
        P(SEC),
        P(SEC, DEV),
        P(DEV),
        P(DEV, SEC),
        P(SEC),
    )
    return jax.shard_map(
        local, mesh=fine, in_specs=in_specs, out_specs=P(None, DEV, SEC), check_vma=False
    )
```

```python
import jax
import jax.numpy as jnp
from jax import lax
from jax.sharding import Mesh, PartitionSpec as P

f32, bf16 = jnp.float32, jnp.bfloat16
NY, NXLO, NXHI, NZ, NCORE = 4, 2, 2, 8, 2
SEC = ("y", "xlo")
DEV = ("xhi", "z", "core")
NEAR = ("xlo", "xhi", "core")


def swap(x, axis):
    return lax.ppermute(x, axis, [(0, 1), (1, 0)])


def turn(x, axis, d):
    n = lax.axis_size(axis)
    pairs = [(i * 2 + c, (i + d * (1 - 2 * c)) % n * 2 + c) for i in range(n) for c in range(2)]
    return lax.ppermute(x, (axis, "core"), pairs)


def near(x, mask):
    return lax.ppermute(x, NEAR, [(i, i ^ mask) for i in range(8)])


def after(x, other):
    return lax.optimization_barrier((x, other))[0]


def ordered(which, own, other):
    first = which == 0
    return jnp.where(first, own, other), jnp.where(first, other, own)


def add(a, b):
    return (a.astype(f32) + b.astype(f32)).astype(bf16)


def ring_sum(down, z, way):
    rows, cols = down.shape[0] // NZ, down.shape[1]
    half = cols // 2

    def block(d):
        return lax.dynamic_slice_in_dim(down, (z + d * way + NZ) % NZ * rows, rows, 0)

    opposite = block(NZ // 2)
    there = turn(opposite[:, :half], "z", 1)
    back = turn(opposite[:, half:], "z", -1)
    for d in range(NZ // 2 - 1, 0, -1):
        a, b = block(d), block(-d)
        if d == NZ // 2 - 1:
            a = jnp.concatenate([add(a[:, :half], there), a[:, half:]], axis=1)
            b = jnp.concatenate([b[:, :half], add(b[:, half:], back)], axis=1)
        else:
            a, b = add(a, there), add(b, back)
        there, back = turn(a, "z", 1), turn(b, "z", -1)
    return block(0).astype(f32) + there.astype(f32) + back.astype(f32)


def ring_gather(first, second, z, way):
    moving = [first, second]
    whole = [[jnp.zeros((NZ,) + m.shape[1:], m.dtype) for _ in range(2)] for m in moving]
    for d in range(NZ):
        if d == 1:
            moving[0] = arrival = turn(moving[0], "z", 1)
            moving[1] = turn(after(moving[1], arrival), "z", 1)
        elif d:
            moving = [turn(m, "z", 1) for m in moving]
        source = (z - d * way + NZ) % NZ
        whole = [
            [lax.dynamic_update_slice_in_dim(w, m[r : r + 1], source, 0) for r, w in enumerate(pair)]
            for pair, m in zip(whole, moving)
        ]
    return whole, arrival


def local(acts, ln_gain, ln_bias, w1, up_bias, w2, down_bias):
    micros, seq, width = acts.shape
    own_seq = seq // (NXHI * NZ * NCORE)
    chunk = NZ * own_seq
    tokens = NXHI * chunk
    y, xlo, xhi, z, core = (lax.axis_index(a) for a in ("y", "xlo", "xhi", "z", "core"))
    features = width * 256
    way = 1 - 2 * core

    tiles = acts.reshape(micros, NXHI, NZ, NCORE, own_seq, width)
    tiles = tiles.transpose(0, 3, 5, 1, 2, 4).reshape(micros, NCORE, width, tokens)
    mine, theirs = ordered(xlo, tiles[0], tiles[1])
    quarter = [ordered(core, part[0], part[1]) for part in (mine, theirs)]

    def arrived(rx, rh, rc):
        piece, mask = quarter[rx][rc], rx * 4 + rh * 2 + rc
        return near(piece, mask) if mask else piece

    pieces = [[[arrived(rx, rh, rc) for rc in range(2)] for rh in range(2)] for rx in range(2)]
    rows = []
    for rx in range(2):
        by_hi = []
        for rh in range(2):
            a, b = ordered(core, *pieces[rx][rh])
            by_hi.append(jnp.concatenate([a, b], axis=0))
        rows.append(jnp.stack(ordered(xhi, *by_hi)))
    x = jnp.stack(rows)

    flat = x.reshape(NXLO, NXHI * 2 * width, tokens)
    gathers, arrival = ring_gather(flat[..., :chunk], flat[..., chunk:], z, way)

    k1, n1 = w1.shape
    w1 = after(w1, pieces[0][0][1])
    scaled = (w1.astype(f32) * ln_gain[:, None]).astype(bf16)
    col = jnp.sum(scaled.astype(f32), axis=0)
    shifted = jnp.sum(w1.astype(f32) * ln_bias[:, None], axis=0)
    vec = jnp.stack([col, shifted])
    vec = vec + swap(vec, "xlo")
    scaled = after(scaled, vec)
    vec = jnp.stack([vec, swap(vec, "core")])

    bias = jnp.concatenate([up_bias, swap(up_bias, "core")])
    scaled = scaled.reshape(NXHI, NZ, 2 * width, n1).transpose(1, 0, 2, 3).reshape(k1, n1)
    scaled = after(scaled, x)
    w1s = [[scaled, swap(scaled, "core")]]
    far = swap(scaled, "xlo")
    w1s.append([far, swap(far, "core")])
    far2 = swap(after(w2, far), "xlo")

    part = chunk // NY

    x32 = after(x, arrival).astype(f32)
    count = x.shape[0] * x.shape[1] * x.shape[2]
    mean = jnp.sum(x32, axis=(0, 1, 2)) / count
    m2 = jnp.sum(jnp.square(x32 - mean), axis=(0, 1, 2))
    every = after(lax.all_gather(jnp.stack([mean, m2]), ("y", "z")), gathers[0])
    mean = jnp.sum(every[:, 0], axis=0) / (NY * NZ)
    m2 = jnp.sum(every[:, 1] + count * jnp.square(every[:, 0] - mean), axis=0)
    mean, rstd = mean[:, None], lax.rsqrt(m2 / features + 1e-05)[:, None]

    def project_up(t, gathered):
        cut = slice(t * chunk, (t + 1) * chunk)
        ups = []
        for j in range(NCORE):
            acc = sum(
                lax.dot_general(
                    gathered[r].reshape(k1, chunk),
                    w1s[r][j],
                    (((0,), (0,)), ((), ())),
                    preferred_element_type=f32,
                )
                for r in range(NXLO)
            )
            ups.append(((acc - mean[cut] * vec[j, 0]) * rstd[cut] + vec[j, 1]).astype(bf16))
        return ups

    def spread(ups):
        def block(d):
            at = (y + d + NY) % NY * part
            return jnp.concatenate(
                [lax.dynamic_slice_in_dim(up, at, part, 0) for up in ups], axis=1
            )

        opposite = turn(block(2), "y", 1)
        near_by = turn(block(-way), "y", -1)
        return [block(0), near_by, turn(add(block(way), opposite), "y", 1)], opposite

    def activate(terms):
        total = sum(term.astype(f32) for term in terms)
        return jax.nn.gelu(total + bias, approximate=True).astype(bf16)

    def share(act):
        first = turn(act, "y", 1)
        return [first, turn(act, "y", -1), turn(first, "y", 1)]

    def project_down(w2_cat, act, others):
        hidden = jnp.zeros((chunk, NCORE * n1), bf16)
        for d, got in zip((0, -way, way, 2), [act] + others):
            hidden = lax.dynamic_update_slice_in_dim(hidden, got, (y + d + NY) % NY * part, 0)
        return jnp.dot(hidden, w2_cat, preferred_element_type=f32).astype(bf16)

    up0 = project_up(0, gathers[0])
    terms0, opposite0 = spread(up0)
    up1 = project_up(1, after(gathers[1], up0))
    terms1, _ = spread(after(up1, opposite0))
    act0 = activate(after(terms0, up1))
    acts0 = share(act0)
    far2 = after(far2, act0)
    w2_cat = jnp.concatenate(
        [
            jnp.concatenate([w2, far2], axis=1),
            jnp.concatenate([swap(w2, "core"), swap(far2, "core")], axis=1),
        ],
        axis=0,
    )
    act1 = activate(after(terms1, act0))
    acts1 = share(act1)
    down0 = project_down(w2_cat, act0, after(acts0, act1))
    outs = [lax.psum_scatter(down0, "z", scatter_dimension=0, tiled=True)]
    down1 = project_down(w2_cat, act1, after(acts1, down0))
    outs.append(ring_sum(down1, z, way).astype(bf16))

    keep, send = ordered(xhi, outs[0], outs[1])
    cols = down_bias.shape[0]
    here = keep[:, :cols].astype(f32) + near(send[:, :cols], 2).astype(f32)
    other = near(keep[:, cols:], 4).astype(f32) + near(send[:, cols:], 6).astype(f32)
    both = jnp.stack(ordered(xlo, here, other))
    return (both + down_bias).astype(bf16)


def solution(mesh):
    fine = Mesh(mesh.devices.reshape(NY, NXLO, NXHI, NZ, NCORE), SEC + DEV)
    in_specs = (
        P(None, None, SEC + DEV),
        P(SEC),
        P(SEC),
        P(SEC, DEV),
        P(DEV),
        P(DEV, SEC),
        P(SEC),
    )
    return jax.shard_map(
        local, mesh=fine, in_specs=in_specs, out_specs=P(None, DEV, SEC), check_vma=False
    )
```

```python
import jax
import jax.numpy as jnp
from jax import lax
from jax.sharding import Mesh, PartitionSpec as P

f32, bf16 = jnp.float32, jnp.bfloat16
NY, NXLO, NXHI, NZ, NCORE = 4, 2, 2, 8, 2
SEC = ("y", "xlo")
DEV = ("xhi", "z", "core")
NEAR = ("xlo", "xhi", "core")


def swap(x, axis):
    return lax.ppermute(x, axis, [(0, 1), (1, 0)])


def turn(x, axis, d):
    n = lax.axis_size(axis)
    pairs = [(i * 2 + c, (i + d * (1 - 2 * c)) % n * 2 + c) for i in range(n) for c in range(2)]
    return lax.ppermute(x, (axis, "core"), pairs)


def near(x, mask):
    return lax.ppermute(x, NEAR, [(i, i ^ mask) for i in range(8)])


def flip(x, axis, bit):
    return lax.ppermute(x, axis, [(i, i ^ bit) for i in range(lax.axis_size(axis))])


def after(x, other):
    return lax.optimization_barrier((x, other))[0]


def ordered(which, own, other):
    first = which == 0
    return jnp.where(first, own, other), jnp.where(first, other, own)


def add(a, b):
    return (a.astype(f32) + b.astype(f32)).astype(bf16)


def ring_sum(down, z, way):
    rows, cols = down.shape[0] // NZ, down.shape[1]
    half = cols // 2

    def block(d):
        return lax.dynamic_slice_in_dim(down, (z + d * way + NZ) % NZ * rows, rows, 0)

    opposite = block(NZ // 2)
    there = turn(opposite[:, :half], "z", 1)
    back = turn(opposite[:, half:], "z", -1)
    for d in range(NZ // 2 - 1, 0, -1):
        a, b = block(d), block(-d)
        if d == NZ // 2 - 1:
            a = jnp.concatenate([add(a[:, :half], there), a[:, half:]], axis=1)
            b = jnp.concatenate([b[:, :half], add(b[:, half:], back)], axis=1)
        else:
            a, b = add(a, there), add(b, back)
        there, back = turn(a, "z", 1), turn(b, "z", -1)
    return block(0).astype(f32) + there.astype(f32) + back.astype(f32)


def ring_gather(first, second, z, way):
    moving = [first, second]
    whole = [[jnp.zeros((NZ,) + m.shape[1:], m.dtype) for _ in range(2)] for m in moving]
    arrivals = [first]
    for d in range(NZ):
        if d == 1:
            moving[0] = turn(moving[0], "z", 1)
            moving[1] = turn(after(moving[1], moving[0]), "z", 1)
        elif d:
            moving = [turn(m, "z", 1) for m in moving]
        arrivals.append(moving[0])
        source = (z - d * way + NZ) % NZ
        whole = [
            [lax.dynamic_update_slice_in_dim(w, m[r : r + 1], source, 0) for r, w in enumerate(pair)]
            for pair, m in zip(whole, moving)
        ]
    return whole, arrivals[1:]


def local(acts, ln_gain, ln_bias, w1, up_bias, w2, down_bias):
    micros, seq, width = acts.shape
    own_seq = seq // (NXHI * NZ * NCORE)
    chunk = NZ * own_seq
    tokens = NXHI * chunk
    y, xlo, xhi, z, core = (lax.axis_index(a) for a in ("y", "xlo", "xhi", "z", "core"))
    features = width * 256
    way = 1 - 2 * core

    tiles = acts.reshape(micros, NXHI, NZ, NCORE, own_seq, width)
    tiles = tiles.transpose(0, 3, 5, 1, 2, 4).reshape(micros, NCORE, width, tokens)
    mine, theirs = ordered(xlo, tiles[0], tiles[1])
    quarter = [ordered(core, part[0], part[1]) for part in (mine, theirs)]

    def arrived(rx, rh, rc):
        piece, mask = quarter[rx][rc], rx * 4 + rh * 2 + rc
        return near(piece, mask) if mask else piece

    pieces = [[[arrived(rx, rh, rc) for rc in range(2)] for rh in range(2)] for rx in range(2)]
    rows = []
    for rx in range(2):
        by_hi = []
        for rh in range(2):
            a, b = ordered(core, *pieces[rx][rh])
            by_hi.append(jnp.concatenate([a, b], axis=0))
        rows.append(jnp.stack(ordered(xhi, *by_hi)))
    x = jnp.stack(rows)

    flat = x.reshape(NXLO, NXHI * 2 * width, tokens)
    gathers, arrivals = ring_gather(flat[..., :chunk], flat[..., chunk:], z, way)

    k1, n1 = w1.shape
    w1 = after(w1, pieces[0][0][1])
    scaled = (w1.astype(f32) * ln_gain[:, None]).astype(bf16)
    col = jnp.sum(scaled.astype(f32), axis=0)
    shifted = jnp.sum(w1.astype(f32) * ln_bias[:, None], axis=0)
    vec = jnp.stack([col, shifted])
    vec = vec + swap(vec, "xlo")
    scaled = after(scaled, vec)
    vec = jnp.stack([vec, swap(vec, "core")])

    scaled = scaled.reshape(NXHI, NZ, 2 * width, n1).transpose(1, 0, 2, 3).reshape(k1, n1)
    scaled = after(scaled, x)
    w1s = [[scaled, swap(scaled, "core")]]
    far = swap(scaled, "xlo")
    w1s.append([far, swap(far, "core")])
    far2 = swap(after(w2, far), "xlo")

    part = chunk // NY

    def join(axis, bit, count, mean, m2, *rest):
        theirs = flip(jnp.concatenate([mean, m2, *rest]), axis, bit)
        m2 = m2 + theirs[1:2] + (count / 2) * jnp.square(mean - theirs[:1])
        mean = (mean + theirs[:1]) / 2
        return 2 * count, mean, m2, *(rest and [rest[0] + theirs[2:]])

    count = x.shape[0] * x.shape[1] * x.shape[2]
    x32 = after(x, arrivals[1]).astype(f32)
    mean = (jnp.sum(x32, axis=(0, 1, 2)) / count)[None]
    m2 = jnp.sum(jnp.square(x32 - mean), axis=(0, 1, 2))[None]
    total_vec = jnp.pad(vec.reshape(2 * NCORE, n1), ((0, 0), (0, tokens - n1)))
    mean = after(mean, arrivals[2])
    count, mean, m2, total_vec = join("y", 1, count, mean, m2, total_vec)
    mean = after(mean, arrivals[4])
    count, mean, m2, total_vec = join("y", 2, count, mean, m2, total_vec)
    pivot = mean.reshape(-1, 1)
    total_vec = total_vec[:, :n1].reshape(vec.shape)
    total_col = total_vec[:, 0].reshape(-1)
    bias = total_vec[:, 1].reshape(-1) + jnp.concatenate([up_bias, swap(up_bias, "core")])

    def project_up(t, gathered):
        base = pivot[t * chunk : (t + 1) * chunk]
        ups = []
        for j in range(NCORE):
            acc = sum(
                lax.dot_general(
                    gathered[r].reshape(k1, chunk),
                    w1s[r][j],
                    (((0,), (0,)), ((), ())),
                    preferred_element_type=f32,
                )
                for r in range(NXLO)
            )
            ups.append((acc - base * vec[j, 0]).astype(bf16))
        return ups

    def spread(ups):
        def block(d):
            at = (y + d + NY) % NY * part
            return jnp.concatenate(
                [lax.dynamic_slice_in_dim(up, at, part, 0) for up in ups], axis=1
            )

        opposite = turn(block(2), "y", 1)
        near_by = turn(block(-way), "y", -1)
        return [block(0), near_by, turn(add(block(way), opposite), "y", 1)], opposite

    def activate(t, terms):
        total = sum(term.astype(f32) for term in terms)
        rows = [lax.dynamic_slice_in_dim(v, t * chunk + y * part, part) for v in (moved, rstd)]
        total = (total + rows[0] * total_col) * rows[1] + bias
        return jax.nn.gelu(total, approximate=True).astype(bf16)

    def share(act):
        first = turn(act, "y", 1)
        return [first, turn(act, "y", -1), turn(first, "y", 1)]

    def project_down(w2_cat, act, others):
        hidden = jnp.zeros((chunk, NCORE * n1), bf16)
        for d, got in zip((0, -way, way, 2), [act] + others):
            hidden = lax.dynamic_update_slice_in_dim(hidden, got, (y + d + NY) % NY * part, 0)
        return jnp.dot(hidden, w2_cat, preferred_element_type=f32).astype(bf16)

    up0 = project_up(0, gathers[0])
    terms0, opposite0 = spread(up0)
    up1 = project_up(1, after(gathers[1], up0))
    terms1, _ = spread(after(up1, opposite0))
    mean, m2 = after((mean, m2), opposite0)
    for bit in (1, 2, 4):
        count, mean, m2 = join("z", bit, count, mean, m2)
    rstd = lax.rsqrt(m2 / features + 1e-05).reshape(-1, 1)
    moved = pivot - mean.reshape(-1, 1)
    act0 = activate(0, after(terms0, up1))
    acts0 = share(act0)
    far2 = after(far2, act0)
    w2_cat = jnp.concatenate(
        [
            jnp.concatenate([w2, far2], axis=1),
            jnp.concatenate([swap(w2, "core"), swap(far2, "core")], axis=1),
        ],
        axis=0,
    )
    act1 = activate(1, after(terms1, act0))
    acts1 = share(act1)
    down0 = project_down(w2_cat, act0, after(acts0, act1))
    outs = [lax.psum_scatter(down0, "z", scatter_dimension=0, tiled=True)]
    down1 = project_down(w2_cat, act1, after(acts1, down0))
    outs.append(ring_sum(down1, z, way).astype(bf16))

    keep, send = ordered(xhi, outs[0], outs[1])
    cols = down_bias.shape[0]
    here = keep[:, :cols].astype(f32) + near(send[:, :cols], 2).astype(f32)
    other = near(keep[:, cols:], 4).astype(f32) + near(send[:, cols:], 6).astype(f32)
    both = jnp.stack(ordered(xlo, here, other))
    return (both + down_bias).astype(bf16)


def solution(mesh):
    fine = Mesh(mesh.devices.reshape(NY, NXLO, NXHI, NZ, NCORE), SEC + DEV)
    in_specs = (
        P(None, None, SEC + DEV),
        P(SEC),
        P(SEC),
        P(SEC, DEV),
        P(DEV),
        P(DEV, SEC),
        P(SEC),
    )
    return jax.shard_map(
        local, mesh=fine, in_specs=in_specs, out_specs=P(None, DEV, SEC), check_vma=False
    )
```

```python
import jax
import jax.numpy as jnp
from jax import lax
from jax.sharding import Mesh, PartitionSpec as P

f32, bf16 = jnp.float32, jnp.bfloat16
NY, NXLO, NXHI, NZ, NCORE = 4, 2, 2, 8, 2
SEC = ("y", "xlo")
DEV = ("xhi", "z", "core")
NEAR = ("xlo", "xhi", "core")


def swap(x, axis):
    return lax.ppermute(x, axis, [(0, 1), (1, 0)])


def turn(x, axis, d):
    n = lax.axis_size(axis)
    pairs = [(i * 2 + c, (i + d * (1 - 2 * c)) % n * 2 + c) for i in range(n) for c in range(2)]
    return lax.ppermute(x, (axis, "core"), pairs)


def near(x, mask):
    return lax.ppermute(x, NEAR, [(i, i ^ mask) for i in range(8)])


def flip(x, axis, bit):
    return lax.ppermute(x, axis, [(i, i ^ bit) for i in range(lax.axis_size(axis))])


def after(x, other):
    return lax.optimization_barrier((x, other))[0]


def ordered(which, own, other):
    first = which == 0
    return jnp.where(first, own, other), jnp.where(first, other, own)


def add(a, b):
    return (a.astype(f32) + b.astype(f32)).astype(bf16)


def ring_sum(down, z, way):
    rows, cols = down.shape[0] // NZ, down.shape[1]
    half = cols // 2

    def block(d):
        return lax.dynamic_slice_in_dim(down, (z + d * way + NZ) % NZ * rows, rows, 0)

    opposite = block(NZ // 2)
    there = turn(opposite[:, :half], "z", 1)
    back = turn(opposite[:, half:], "z", -1)
    for d in range(NZ // 2 - 1, 0, -1):
        a, b = block(d), block(-d)
        if d == NZ // 2 - 1:
            a = jnp.concatenate([add(a[:, :half], there), a[:, half:]], axis=1)
            b = jnp.concatenate([b[:, :half], add(b[:, half:], back)], axis=1)
        else:
            a, b = add(a, there), add(b, back)
        there, back = turn(a, "z", 1), turn(b, "z", -1)
    return block(0).astype(f32) + there.astype(f32) + back.astype(f32)


def ring_gather(first, second, z, way):
    moving = [first, second]
    whole = [[jnp.zeros((NZ,) + m.shape[1:], m.dtype) for _ in range(2)] for m in moving]
    arrivals = [first]
    for d in range(NZ):
        if d:
            moving = [turn(m, "z", 1) for m in moving]
        arrivals.append(moving[0])
        source = (z - d * way + NZ) % NZ
        whole = [
            [lax.dynamic_update_slice_in_dim(w, m[r : r + 1], source, 0) for r, w in enumerate(pair)]
            for pair, m in zip(whole, moving)
        ]
    return whole, arrivals[1:]


def local(acts, ln_gain, ln_bias, w1, up_bias, w2, down_bias):
    micros, seq, width = acts.shape
    own_seq = seq // (NXHI * NZ * NCORE)
    chunk = NZ * own_seq
    tokens = NXHI * chunk
    y, xlo, xhi, z, core = (lax.axis_index(a) for a in ("y", "xlo", "xhi", "z", "core"))
    features = width * 256
    way = 1 - 2 * core

    tiles = acts.reshape(micros, NXHI, NZ, NCORE, own_seq, width)
    tiles = tiles.transpose(0, 3, 5, 1, 2, 4).reshape(micros, NCORE, width, tokens)
    mine, theirs = ordered(xlo, tiles[0], tiles[1])
    quarter = [ordered(core, part[0], part[1]) for part in (mine, theirs)]

    def arrived(rx, rh, rc):
        piece, mask = quarter[rx][rc], rx * 4 + rh * 2 + rc
        return near(piece, mask) if mask else piece

    pieces = [[[arrived(rx, rh, rc) for rc in range(2)] for rh in range(2)] for rx in range(2)]
    rows = []
    for rx in range(2):
        by_hi = []
        for rh in range(2):
            a, b = ordered(core, *pieces[rx][rh])
            by_hi.append(jnp.concatenate([a, b], axis=0))
        rows.append(jnp.stack(ordered(xhi, *by_hi)))
    x = jnp.stack(rows)

    flat = x.reshape(NXLO, NXHI * 2 * width, tokens)
    gathers, arrivals = ring_gather(flat[..., :chunk], flat[..., chunk:], z, way)

    k1, n1 = w1.shape
    w1 = after(w1, pieces[0][0][1])
    scaled = (w1.astype(f32) * ln_gain[:, None]).astype(bf16)
    col = jnp.sum(scaled.astype(f32), axis=0)
    shifted = jnp.sum(w1.astype(f32) * ln_bias[:, None], axis=0)
    vec = jnp.stack([col, shifted])
    vec = vec + swap(vec, "xlo")
    scaled = after(scaled, vec)
    vec = jnp.concatenate([vec, swap(vec, "core")])
    scaled = scaled.reshape(NXHI, NZ, 2 * width, n1).transpose(1, 0, 2, 3).reshape(k1, n1)
    scaled = after(scaled, x)
    w1s = [[scaled, swap(scaled, "core")]]
    far = swap(scaled, "xlo")
    w1s.append([far, swap(far, "core")])
    far2 = swap(after(w2, far), "xlo")

    part = chunk // NY

    def join(axis, bit, count, mean, m2):
        theirs = flip(jnp.concatenate([mean, m2]), axis, bit)
        m2 = m2 + theirs[1:] + (count / 2) * jnp.square(mean - theirs[:1])
        return 2 * count, (mean + theirs[:1]) / 2, m2

    count = x.shape[0] * x.shape[1] * x.shape[2]
    x32 = after(x, arrivals[1]).astype(f32)
    mean = (jnp.sum(x32, axis=(0, 1, 2)) / count)[None]
    m2 = jnp.sum(jnp.square(x32 - mean), axis=(0, 1, 2))[None]
    for bit, at in ((1, 2), (2, 3)):
        count, mean, m2 = join("y", bit, count, after(mean, arrivals[at]), m2)
    pivot = mean.reshape(-1, 1)
    total_vec = vec
    for bit, at in ((1, 4), (2, 5)):
        total_vec = after(total_vec, arrivals[at])
        total_vec = total_vec + flip(total_vec, "y", bit)
    up_biases = [up_bias[None], swap(up_bias[None], "core")]

    def project_up(t, gathered):
        base = pivot[t * chunk : (t + 1) * chunk]
        ups = []
        for j in range(NCORE):
            acc = sum(
                lax.dot_general(
                    gathered[r].reshape(k1, chunk),
                    w1s[r][j],
                    (((0,), (0,)), ((), ())),
                    preferred_element_type=f32,
                )
                for r in range(NXLO)
            )
            ups.append((acc - base * vec[2 * j]).astype(bf16))
        return ups

    def spread(ups):
        def block(d):
            at = (y + d + NY) % NY * part
            return jnp.concatenate(
                [lax.dynamic_slice_in_dim(up, at, part, 0) for up in ups], axis=1
            )

        opposite = turn(block(2), "y", 1)
        near_by = turn(block(-way), "y", -1)
        return [block(0), near_by, turn(add(block(way), opposite), "y", 1)], opposite

    def activate(t, terms, total_col, bias, moved, rstd):
        total = sum(term.astype(f32) for term in terms)
        rows = [lax.dynamic_slice_in_dim(v, t * chunk + y * part, part) for v in (moved, rstd)]
        total = (total + rows[0] * total_col) * rows[1] + bias
        return jax.nn.gelu(total, approximate=True).astype(bf16)

    def share(act):
        first = turn(act, "y", 1)
        return [first, turn(act, "y", -1), turn(first, "y", 1)]

    def project_down(w2_cat, act, others):
        hidden = jnp.zeros((chunk, NCORE * n1), bf16)
        for d, got in zip((0, -way, way, 2), [act] + others):
            hidden = lax.dynamic_update_slice_in_dim(hidden, got, (y + d + NY) % NY * part, 0)
        return jnp.dot(hidden, w2_cat, preferred_element_type=f32).astype(bf16)

    up0 = project_up(0, gathers[0])
    terms0, opposite0 = spread(up0)
    up1 = project_up(1, after(gathers[1], up0))
    terms1, _ = spread(after(up1, opposite0))
    mean, m2 = after((mean, m2), opposite0)
    for bit in (1, 2, 4):
        count, mean, m2 = join("z", bit, count, mean, m2)
    rstd = lax.rsqrt(m2 / features + 1e-05).reshape(-1, 1)
    moved = pivot - mean.reshape(-1, 1)
    total_vec = after(total_vec, opposite0)
    total_col = jnp.concatenate([total_vec[2 * j : 2 * j + 1] for j in range(NCORE)], axis=1)
    bias = jnp.concatenate(
        [total_vec[2 * j + 1 : 2 * j + 2] + up_biases[j] for j in range(NCORE)], axis=1
    )
    act0 = activate(0, after(terms0, up1), total_col, bias, moved, rstd)
    acts0 = share(act0)
    far2 = after(far2, act0)
    w2_cat = jnp.concatenate(
        [
            jnp.concatenate([w2, far2], axis=1),
            jnp.concatenate([swap(w2, "core"), swap(far2, "core")], axis=1),
        ],
        axis=0,
    )
    act1 = activate(1, after(terms1, act0), total_col, bias, moved, rstd)
    acts1 = share(act1)
    down0 = project_down(w2_cat, act0, after(acts0, act1))
    outs = [lax.psum_scatter(down0, "z", scatter_dimension=0, tiled=True)]
    down1 = project_down(w2_cat, act1, after(acts1, down0))
    outs.append(ring_sum(down1, z, way).astype(bf16))

    keep, send = ordered(xhi, outs[0], outs[1])
    cols = down_bias.shape[0]
    here = keep[:, :cols].astype(f32) + near(send[:, :cols], 2).astype(f32)
    other = near(keep[:, cols:], 4).astype(f32) + near(send[:, cols:], 6).astype(f32)
    both = jnp.stack(ordered(xlo, here, other))
    return (both + down_bias).astype(bf16)


def solution(mesh):
    fine = Mesh(mesh.devices.reshape(NY, NXLO, NXHI, NZ, NCORE), SEC + DEV)
    in_specs = (
        P(None, None, SEC + DEV),
        P(SEC),
        P(SEC),
        P(SEC, DEV),
        P(DEV),
        P(DEV, SEC),
        P(SEC),
    )
    return jax.shard_map(
        local, mesh=fine, in_specs=in_specs, out_specs=P(None, DEV, SEC), check_vma=False
    )
```

```python
import jax
import jax.numpy as jnp
from jax import lax
from jax.sharding import Mesh, PartitionSpec as P

f32, bf16 = jnp.float32, jnp.bfloat16
NY, NXLO, NXHI, NZ, NCORE = 4, 2, 2, 8, 2
SEC = ("y", "xlo")
DEV = ("xhi", "z", "core")
NEAR = ("xlo", "xhi", "core")


def swap(x, axis):
    return lax.ppermute(x, axis, [(0, 1), (1, 0)])


def turn(x, axis, d):
    n = lax.axis_size(axis)
    pairs = [(i * 2 + c, (i + d * (1 - 2 * c)) % n * 2 + c) for i in range(n) for c in range(2)]
    return lax.ppermute(x, (axis, "core"), pairs)


def near(x, mask):
    return lax.ppermute(x, NEAR, [(i, i ^ mask) for i in range(8)])


def flip(x, axis, bit):
    return lax.ppermute(x, axis, [(i, i ^ bit) for i in range(lax.axis_size(axis))])


def after(x, other):
    return lax.optimization_barrier((x, other))[0]


def ordered(which, own, other):
    first = which == 0
    return jnp.where(first, own, other), jnp.where(first, other, own)


def add(a, b):
    return (a.astype(f32) + b.astype(f32)).astype(bf16)


def ring_sum(down, z, way):
    rows, cols = down.shape[0] // NZ, down.shape[1]
    half = cols // 2

    def block(d):
        return lax.dynamic_slice_in_dim(down, (z + d * way + NZ) % NZ * rows, rows, 0)

    opposite = block(NZ // 2)
    there = turn(opposite[:, :half], "z", 1)
    back = turn(opposite[:, half:], "z", -1)
    for d in range(NZ // 2 - 1, 0, -1):
        a, b = block(d), block(-d)
        if d == NZ // 2 - 1:
            a = jnp.concatenate([add(a[:, :half], there), a[:, half:]], axis=1)
            b = jnp.concatenate([b[:, :half], add(b[:, half:], back)], axis=1)
        else:
            a, b = add(a, there), add(b, back)
        there, back = turn(a, "z", 1), turn(b, "z", -1)
    return block(0).astype(f32) + there.astype(f32) + back.astype(f32)


def local(acts, ln_gain, ln_bias, w1, up_bias, w2, down_bias):
    micros, seq, width = acts.shape
    own_seq = seq // (NXHI * NZ * NCORE)
    first_rows = own_seq * 5 // 8
    cuts = [(0, first_rows), (first_rows, own_seq)]
    tokens = NXHI * NZ * own_seq
    y, xlo, xhi, z, core = (lax.axis_index(a) for a in ("y", "xlo", "xhi", "z", "core"))
    features = width * 256
    way = 1 - 2 * core

    tiles = acts.reshape(micros, NXHI, NZ, NCORE, own_seq, width).transpose(0, 3, 2, 1, 4, 5)
    tiles = jnp.concatenate(
        [tiles[..., i:j, :].reshape(micros, NCORE, -1, width) for i, j in cuts], axis=2
    )
    tiles = tiles.transpose(0, 1, 3, 2)
    mine, theirs = ordered(xlo, tiles[0], tiles[1])
    quarter = [ordered(core, part[0], part[1]) for part in (mine, theirs)]

    def arrived(rx, rh, rc):
        piece, mask = quarter[rx][rc], rx * 4 + rh * 2 + rc
        return near(piece, mask) if mask else piece

    pieces = [[[arrived(rx, rh, rc) for rc in range(2)] for rh in range(2)] for rx in range(2)]
    rows = []
    for rx in range(2):
        by_hi = []
        for rh in range(2):
            a, b = ordered(core, *pieces[rx][rh])
            by_hi.append(jnp.concatenate([a, b], axis=0))
        rows.append(jnp.stack(ordered(xhi, *by_hi)))
    x = jnp.stack(rows)

    k1, n1 = w1.shape
    w1 = after(w1, pieces[0][0][1])
    scaled = (w1.astype(f32) * ln_gain[:, None]).astype(bf16)
    col = jnp.sum(scaled.astype(f32), axis=0)
    shifted = jnp.sum(w1.astype(f32) * ln_bias[:, None], axis=0)
    vec = jnp.stack([col, shifted])
    vec = vec + swap(vec, "xlo")
    x, scaled = lax.optimization_barrier((x, after(scaled, vec)))
    vec = jnp.concatenate([vec, swap(vec, "core")])

    scaled = scaled.reshape(NXHI, NZ, 2 * width, n1).transpose(1, 0, 2, 3).reshape(k1, n1)
    w1s = [[scaled, swap(scaled, "core")]]
    far = swap(scaled, "xlo")
    w1s.append([far, swap(far, "core")])
    far2 = swap(after(w2, far), "xlo")

    spans = [(NXHI * NZ * i, NXHI * NZ * j) for i, j in cuts]
    gathers = [lax.all_gather(x[..., i:j], "z") for i, j in spans]

    count = x.shape[0] * x.shape[1] * x.shape[2]
    x32 = x.astype(f32)
    mean = (jnp.sum(x32, axis=(0, 1, 2)) / count)[None]
    m2 = jnp.sum(jnp.square(x32 - mean), axis=(0, 1, 2))[None]
    for axis, bit in (("y", 1), ("y", 2), ("z", 1), ("z", 2), ("z", 4)):
        theirs = flip(jnp.concatenate([mean, m2]), axis, bit)
        m2 = m2 + theirs[1:] + (count / 2) * jnp.square(mean - theirs[:1])
        mean, count = (mean + theirs[:1]) / 2, 2 * count
    mean, rstd = mean.reshape(-1, 1), lax.rsqrt(m2 / features + 1e-05).reshape(-1, 1)
    bias = jnp.concatenate([up_bias[None], swap(up_bias[None], "core")], axis=1)

    def project_up(t, gathered):
        cut = slice(*spans[t])
        ups = []
        for j in range(NCORE):
            acc = sum(
                lax.dot_general(
                    gathered[:, r].reshape(k1, -1),
                    w1s[r][j],
                    (((0,), (0,)), ((), ())),
                    preferred_element_type=f32,
                )
                for r in range(NXLO)
            )
            up = (acc - mean[cut] * vec[2 * j]) * rstd[cut] + vec[2 * j + 1]
            ups.append(up.astype(bf16))
        return ups

    def spread(ups):
        part = ups[0].shape[0] // NY

        def block(d):
            at = (y + d + NY) % NY * part
            return jnp.concatenate(
                [lax.dynamic_slice_in_dim(up, at, part, 0) for up in ups], axis=1
            )

        opposite = turn(block(2), "y", 1)
        near_by = turn(block(-way), "y", -1)
        return [block(0), near_by, turn(add(block(way), opposite), "y", 1)], opposite

    def activate(terms):
        total = sum(term.astype(f32) for term in terms)
        return jax.nn.gelu(total + bias, approximate=True).astype(bf16)

    def share(act):
        first = turn(act, "y", 1)
        return [first, turn(act, "y", -1), turn(first, "y", 1)]

    def project_down(w2_cat, act, others):
        part = act.shape[0]
        hidden = jnp.zeros((NY * part, NCORE * n1), bf16)
        for d, got in zip((0, -way, way, 2), [act] + others):
            hidden = lax.dynamic_update_slice_in_dim(hidden, got, (y + d + NY) % NY * part, 0)
        return jnp.dot(hidden, w2_cat, preferred_element_type=f32).astype(bf16)

    up0 = project_up(0, gathers[0])
    terms0, _ = spread(up0)
    act0 = activate(terms0)
    acts0 = share(act0)
    up1 = project_up(1, after(gathers[1], act0))
    terms1, opposite1 = spread(up1)
    far2 = after(far2, act0)
    w2_cat = jnp.concatenate(
        [
            jnp.concatenate([w2, far2], axis=1),
            jnp.concatenate([swap(w2, "core"), swap(far2, "core")], axis=1),
        ],
        axis=0,
    )
    down0 = project_down(w2_cat, act0, after(acts0, (up1, opposite1)))
    outs = [lax.psum_scatter(down0, "z", scatter_dimension=0, tiled=True)]
    act1 = activate(terms1[:1] + after(terms1[1:], down0))
    down1 = project_down(w2_cat, act1, share(act1))
    outs.append(ring_sum(down1, z, way).astype(bf16))

    halves = [ordered(xhi, *jnp.split(out, NXHI)) for out in outs]
    keep, send = (jnp.concatenate(rows, axis=0) for rows in zip(*halves))
    cols = down_bias.shape[0]
    here = keep[:, :cols].astype(f32) + near(send[:, :cols], 2).astype(f32)
    other = near(keep[:, cols:], 4).astype(f32) + near(send[:, cols:], 6).astype(f32)
    both = jnp.stack(ordered(xlo, here, other))
    return (both + down_bias).astype(bf16)


def solution(mesh):
    fine = Mesh(mesh.devices.reshape(NY, NXLO, NXHI, NZ, NCORE), SEC + DEV)
    in_specs = (
        P(None, None, SEC + DEV),
        P(SEC),
        P(SEC),
        P(SEC, DEV),
        P(DEV),
        P(DEV, SEC),
        P(SEC),
    )
    return jax.shard_map(
        local, mesh=fine, in_specs=in_specs, out_specs=P(None, DEV, SEC), check_vma=False
    )
```

```python
import jax
import jax.numpy as jnp
from jax import lax
from jax.sharding import Mesh, PartitionSpec as P

f32, bf16 = jnp.float32, jnp.bfloat16
NY, NXLO, NXHI, NZ, NCORE = 4, 2, 2, 8, 2
SEC = ("y", "xlo")
DEV = ("xhi", "z", "core")
NEAR = ("xlo", "xhi", "core")


def swap(x, axis):
    return lax.ppermute(x, axis, [(0, 1), (1, 0)])


def turn(x, axis, d):
    n = lax.axis_size(axis)
    pairs = [(i * 2 + c, (i + d * (1 - 2 * c)) % n * 2 + c) for i in range(n) for c in range(2)]
    return lax.ppermute(x, (axis, "core"), pairs)


def near(x, mask):
    return lax.ppermute(x, NEAR, [(i, i ^ mask) for i in range(8)])


def flip(x, axis, bit):
    return lax.ppermute(x, axis, [(i, i ^ bit) for i in range(lax.axis_size(axis))])


def after(x, other):
    return lax.optimization_barrier((x, other))[0]


def ordered(which, own, other):
    first = which == 0
    return jnp.where(first, own, other), jnp.where(first, other, own)


def add(a, b):
    return (a.astype(f32) + b.astype(f32)).astype(bf16)


def ring_sum(down, z, way):
    rows, cols = down.shape[0] // NZ, down.shape[1]
    half = cols // 2

    def block(d):
        return lax.dynamic_slice_in_dim(down, (z + d * way + NZ) % NZ * rows, rows, 0)

    opposite = block(NZ // 2)
    there = turn(opposite[:, :half], "z", 1)
    back = turn(opposite[:, half:], "z", -1)
    for d in range(NZ // 2 - 1, 0, -1):
        a, b = block(d), block(-d)
        if d == NZ // 2 - 1:
            a = jnp.concatenate([add(a[:, :half], there), a[:, half:]], axis=1)
            b = jnp.concatenate([b[:, :half], add(b[:, half:], back)], axis=1)
        else:
            a, b = add(a, there), add(b, back)
        there, back = turn(a, "z", 1), turn(b, "z", -1)
    return block(0).astype(f32) + there.astype(f32) + back.astype(f32)


def local(acts, ln_gain, ln_bias, w1, up_bias, w2, down_bias):
    micros, seq, width = acts.shape
    own_seq = seq // (NXHI * NZ * NCORE)
    first_rows = own_seq * 5 // 8
    cuts = [(0, first_rows), (first_rows, own_seq)]
    tokens = NXHI * NZ * own_seq
    y, xlo, xhi, z, core = (lax.axis_index(a) for a in ("y", "xlo", "xhi", "z", "core"))
    features = width * 256
    way = 1 - 2 * core

    tiles = acts.reshape(micros, NXHI, NZ, NCORE, own_seq, width).transpose(0, 3, 2, 1, 4, 5)
    tiles = jnp.concatenate(
        [tiles[..., i:j, :].reshape(micros, NCORE, -1, width) for i, j in cuts], axis=2
    )
    tiles = tiles.transpose(0, 1, 3, 2)
    mine, theirs = ordered(xlo, tiles[0], tiles[1])
    quarter = [ordered(core, part[0], part[1]) for part in (mine, theirs)]

    def arrived(rx, rh, rc):
        piece, mask = quarter[rx][rc], rx * 4 + rh * 2 + rc
        return near(piece, mask) if mask else piece

    pieces = [[[arrived(rx, rh, rc) for rc in range(2)] for rh in range(2)] for rx in range(2)]
    rows = []
    for rx in range(2):
        by_hi = []
        for rh in range(2):
            a, b = ordered(core, *pieces[rx][rh])
            by_hi.append(jnp.concatenate([a, b], axis=0))
        rows.append(jnp.stack(ordered(xhi, *by_hi)))
    x = jnp.stack(rows)

    k1, n1 = w1.shape
    w1 = after(w1, pieces[0][0][1])
    scaled = (w1.astype(f32) * ln_gain[:, None]).astype(bf16)
    col = jnp.sum(scaled.astype(f32), axis=0)
    shifted = jnp.sum(w1.astype(f32) * ln_bias[:, None], axis=0)
    vec = jnp.stack([col, shifted])
    vec = vec + swap(vec, "xlo")
    x, scaled = lax.optimization_barrier((x, after(scaled, vec)))
    vecs = [vec, swap(vec, "core")]

    scaled = scaled.reshape(NXHI, NZ, 2 * width, n1).transpose(1, 0, 2, 3)
    scaled = scaled.reshape(NZ, 1, NXHI * 2 * width, n1)
    far = swap(scaled, "xlo")

    def interleave(own, other):
        both = jnp.zeros((NZ, NXLO) + own.shape[2:], own.dtype)
        both = lax.dynamic_update_slice_in_dim(both, own, 0, 1)
        return lax.dynamic_update_slice_in_dim(both, other, 1, 1).reshape(-1, n1)


    spans = [(NXHI * NZ * i, NXHI * NZ * j) for i, j in cuts]
    gathers = [lax.all_gather(x[..., i:j], "z") for i, j in spans]

    count = x.shape[0] * x.shape[1] * x.shape[2]
    x32 = x.astype(f32)
    mean = (jnp.sum(x32, axis=(0, 1, 2)) / count)[None]
    m2 = jnp.sum(jnp.square(x32 - mean), axis=(0, 1, 2))[None]
    scaled_other = swap(scaled, "core")
    mean = after(mean, (vecs[1], scaled_other))
    for axis, bit in (("y", 1), ("y", 2), ("z", 1), ("z", 2), ("z", 4)):
        theirs = flip(jnp.concatenate([mean, m2]), axis, bit)
        m2 = m2 + theirs[1:] + (count / 2) * jnp.square(mean - theirs[:1])
        mean, count = (mean + theirs[:1]) / 2, 2 * count
    mean, rstd = mean.reshape(-1, 1), lax.rsqrt(m2 / features + 1e-05).reshape(-1, 1)
    far = after(far, m2)
    w1s = [scaled, far], [scaled_other, swap(far, "core")]
    far2 = swap(after(w2, far), "xlo")
    bias = jnp.concatenate([up_bias[None], swap(up_bias[None], "core")], axis=1)

    def project_up(t, j, gathered, weights):
        cut = slice(*spans[t])
        acc = lax.dot_general(
            gathered.reshape(-1, gathered.shape[-1]),
            weights,
            (((0,), (0,)), ((), ())),
            preferred_element_type=f32,
        )
        return ((acc - mean[cut] * vecs[j][0]) * rstd[cut] + vecs[j][1]).astype(bf16)

    def spread(ups):
        part = ups[0].shape[0] // NY

        def block(d):
            at = (y + d + NY) % NY * part
            return jnp.concatenate(
                [lax.dynamic_slice_in_dim(up, at, part, 0) for up in ups], axis=1
            )

        return [block(0), turn(block(2), "y", 2)] + [
            turn(block(d * way), "y", d) for d in (1, -1)
        ]

    def activate(terms):
        total = sum(term.astype(f32) for term in terms)
        return jax.nn.gelu(total + bias, approximate=True).astype(bf16)

    def share(act):
        return [turn(act, "y", d) for d in (2, 1, -1)]

    def project_down(w2_cat, act, others):
        part = act.shape[0]
        hidden = jnp.zeros((NY * part, NCORE * n1), bf16)
        for d, got in zip((0, 2, -way, way), [act] + others):
            hidden = lax.dynamic_update_slice_in_dim(hidden, got, (y + d + NY) % NY * part, 0)
        return jnp.dot(hidden, w2_cat, preferred_element_type=f32).astype(bf16)

    weights = [interleave(*w1s[0])]
    up0 = [project_up(0, 0, gathers[0], weights[0])]
    weights.append(interleave(w1s[1][0], after(w1s[1][1], up0[0])))
    up0.append(project_up(0, 1, gathers[0], weights[1]))
    terms0 = spread(up0)
    act0 = activate(terms0)
    acts0 = share(act0)
    gathered1 = after(gathers[1], act0)
    up1 = [project_up(1, 0, gathered1, weights[0])]
    up1.append(project_up(1, 1, after(gathered1, (up1[0], acts0[1])), weights[1]))
    terms1 = spread(up1)
    far2 = after(far2, act0)
    w2_cat = jnp.concatenate(
        [
            jnp.concatenate([w2, far2], axis=1),
            jnp.concatenate([swap(w2, "core"), swap(far2, "core")], axis=1),
        ],
        axis=0,
    )
    down0 = project_down(w2_cat, act0, after(acts0, (up1, terms1[2])))
    outs = [lax.psum_scatter(down0, "z", scatter_dimension=0, tiled=True)]
    act1 = activate(terms1[:1] + after(terms1[1:], down0))
    down1 = project_down(w2_cat, act1, share(act1))
    outs.append(ring_sum(down1, z, way).astype(bf16))

    halves = [ordered(xhi, *jnp.split(out, NXHI)) for out in outs]
    keep, send = (jnp.concatenate(rows, axis=0) for rows in zip(*halves))
    cols = down_bias.shape[0]
    here = keep[:, :cols].astype(f32) + near(send[:, :cols], 2).astype(f32)
    other = near(keep[:, cols:], 4).astype(f32) + near(send[:, cols:], 6).astype(f32)
    both = jnp.stack(ordered(xlo, here, other))
    return (both + down_bias).astype(bf16)


def solution(mesh):
    fine = Mesh(mesh.devices.reshape(NY, NXLO, NXHI, NZ, NCORE), SEC + DEV)
    in_specs = (
        P(None, None, SEC + DEV),
        P(SEC),
        P(SEC),
        P(SEC, DEV),
        P(DEV),
        P(DEV, SEC),
        P(SEC),
    )
    return jax.shard_map(
        local, mesh=fine, in_specs=in_specs, out_specs=P(None, DEV, SEC), check_vma=False
    )
```

```python
import jax
import jax.numpy as jnp
from jax import lax
from jax.sharding import Mesh, PartitionSpec as P

f32, bf16 = jnp.float32, jnp.bfloat16
NY, NXLO, NXHI, NZ, NCORE = 4, 2, 2, 8, 2
SEC = ("y", "xlo")
DEV = ("xhi", "z", "core")
NEAR = ("xlo", "xhi", "core")


def swap(x, axis):
    return lax.ppermute(x, axis, [(0, 1), (1, 0)])


def turn(x, axis, d):
    n = lax.axis_size(axis)
    pairs = [(i * 2 + c, (i + d * (1 - 2 * c)) % n * 2 + c) for i in range(n) for c in range(2)]
    return lax.ppermute(x, (axis, "core"), pairs)


def near(x, mask):
    return lax.ppermute(x, NEAR, [(i, i ^ mask) for i in range(8)])


def flip(x, axis, bit):
    return lax.ppermute(x, axis, [(i, i ^ bit) for i in range(lax.axis_size(axis))])


def after(x, other):
    return lax.optimization_barrier((x, other))[0]


def ordered(which, own, other):
    first = which == 0
    return jnp.where(first, own, other), jnp.where(first, other, own)


def add(a, b):
    return (a.astype(f32) + b.astype(f32)).astype(bf16)


def ring_sum(down, z, way):
    rows, cols = down.shape[0] // NZ, down.shape[1]
    half = cols // 2

    def block(d):
        return lax.dynamic_slice_in_dim(down, (z + d * way + NZ) % NZ * rows, rows, 0)

    opposite = block(NZ // 2)
    there = turn(opposite[:, :half], "z", 1)
    back = turn(opposite[:, half:], "z", -1)
    for d in range(NZ // 2 - 1, 0, -1):
        a, b = block(d), block(-d)
        if d == NZ // 2 - 1:
            a = jnp.concatenate([add(a[:, :half], there), a[:, half:]], axis=1)
            b = jnp.concatenate([b[:, :half], add(b[:, half:], back)], axis=1)
        else:
            a, b = add(a, there), add(b, back)
        there, back = turn(a, "z", 1), turn(b, "z", -1)
    return block(0).astype(f32) + there.astype(f32) + back.astype(f32)


def local(acts, ln_gain, ln_bias, w1, up_bias, w2, down_bias):
    micros, seq, width = acts.shape
    own_seq = seq // (NXHI * NZ * NCORE)
    chunk = NZ * own_seq
    tokens = NXHI * chunk
    y, xlo, xhi, z, core = (lax.axis_index(a) for a in ("y", "xlo", "xhi", "z", "core"))
    features = width * 256
    way = 1 - 2 * core

    tiles = acts.reshape(micros, NXHI, NZ, NCORE, own_seq, width)
    tiles = tiles.transpose(0, 3, 5, 1, 2, 4).reshape(micros, NCORE, width, tokens)
    mine, theirs = ordered(xlo, tiles[0], tiles[1])
    quarter = [ordered(core, part[0], part[1]) for part in (mine, theirs)]

    def arrived(rx, rh, rc):
        piece, mask = quarter[rx][rc], rx * 4 + rh * 2 + rc
        return near(piece, mask) if mask else piece

    pieces = [[[arrived(rx, rh, rc) for rc in range(2)] for rh in range(2)] for rx in range(2)]
    rows = []
    for rx in range(2):
        by_hi = []
        for rh in range(2):
            a, b = ordered(core, *pieces[rx][rh])
            by_hi.append(jnp.concatenate([a, b], axis=0))
        rows.append(jnp.stack(ordered(xhi, *by_hi)))
    x = jnp.stack(rows)

    k1, n1 = w1.shape
    w1 = after(w1, pieces[0][0][1])
    scaled = (w1.astype(f32) * ln_gain[:, None]).astype(bf16)
    col = jnp.sum(scaled.astype(f32), axis=0)
    shifted = jnp.sum(w1.astype(f32) * ln_bias[:, None], axis=0)
    vec = jnp.stack([col, shifted])
    vec = vec + swap(vec, "xlo")
    x, scaled = lax.optimization_barrier((x, after(scaled, vec)))
    vecs = [vec, swap(vec, "core")]

    scaled = scaled.reshape(NXHI, NZ, 2 * width, n1).transpose(1, 0, 2, 3).reshape(k1, n1)
    far = swap(scaled, "xlo")
    scaled_other = swap(scaled, "core")

    spans = [(t * chunk, (t + 1) * chunk) for t in range(NXHI)]
    gathers = [lax.all_gather(x[..., i:j], "z") for i, j in spans]

    count = x.shape[0] * x.shape[1] * x.shape[2]
    x32 = x.astype(f32)
    mean = (jnp.sum(x32, axis=(0, 1, 2)) / count)[None]
    m2 = jnp.sum(jnp.square(x32 - mean), axis=(0, 1, 2))[None]
    mean = after(mean, (vecs[1], scaled_other))
    for axis, bit in (("y", 1), ("y", 2), ("z", 1), ("z", 2), ("z", 4)):
        theirs = flip(jnp.concatenate([mean, m2]), axis, bit)
        m2 = m2 + theirs[1:] + (count / 2) * jnp.square(mean - theirs[:1])
        mean, count = (mean + theirs[:1]) / 2, 2 * count
    mean, rstd = mean.reshape(-1, 1), lax.rsqrt(m2 / features + 1e-05).reshape(-1, 1)
    far = after(far, m2)
    far2 = swap(after(w2, far), "xlo")
    bias = jnp.concatenate([up_bias[None], swap(up_bias[None], "core")], axis=1)

    def project_up(t, j, xs, ws):
        cut = slice(*spans[t])
        acc = sum(
            lax.dot_general(g, w, (((0,), (0,)), ((), ())), preferred_element_type=f32)
            for g, w in zip(xs, ws)
        )
        return ((acc - mean[cut] * vecs[j][0]) * rstd[cut] + vecs[j][1]).astype(bf16)

    def by_section(gathered):
        return [gathered[:, r].reshape(k1, -1) for r in range(NXLO)]

    def spread(ups):
        part = ups[0].shape[0] // NY

        def block(d):
            at = (y + d + NY) % NY * part
            return jnp.concatenate(
                [lax.dynamic_slice_in_dim(up, at, part, 0) for up in ups], axis=1
            )

        return [block(0), turn(block(2), "y", 2)] + [
            turn(block(d * way), "y", d) for d in (1, -1)
        ]

    def activate(terms):
        total = sum(term.astype(f32) for term in terms)
        return jax.nn.gelu(total + bias, approximate=True).astype(bf16)

    def share(act):
        return [turn(act, "y", d) for d in (2, 1, -1)]

    def project_down(w2_cat, act, others):
        part = act.shape[0]
        hidden = jnp.zeros((NY * part, NCORE * n1), bf16)
        for d, got in zip((0, 2, -way, way), [act] + others):
            hidden = lax.dynamic_update_slice_in_dim(hidden, got, (y + d + NY) % NY * part, 0)
        return jnp.dot(hidden, w2_cat, preferred_element_type=f32).astype(bf16)

    xs0 = by_section(gathers[0])
    up0 = [project_up(0, 0, xs0, (scaled, far))]
    far_other = after(swap(far, "core"), up0[0])
    up0.append(project_up(0, 1, xs0, (scaled_other, far_other)))
    terms0 = spread(up0)
    act0 = activate(terms0)
    acts0 = share(act0)
    xs1 = by_section(after(gathers[1], act0))
    up1 = [project_up(1, 0, xs1, (scaled, far))]
    up1.append(project_up(1, 1, after(xs1, (up1[0], acts0[0])), (scaled_other, far_other)))
    terms1 = spread(up1)
    far2 = after(far2, act0)
    w2_cat = jnp.concatenate(
        [
            jnp.concatenate([w2, far2], axis=1),
            jnp.concatenate([swap(w2, "core"), swap(far2, "core")], axis=1),
        ],
        axis=0,
    )
    down0 = project_down(w2_cat, act0, after(acts0, (up1, terms1[2])))
    outs = [lax.psum_scatter(down0, "z", scatter_dimension=0, tiled=True)]
    act1 = activate(terms1[:1] + after(terms1[1:], down0))
    down1 = project_down(w2_cat, act1, share(act1))
    outs.append(ring_sum(down1, z, way).astype(bf16))

    keep, send = ordered(xhi, outs[0], outs[1])
    cols = down_bias.shape[0]
    here = keep[:, :cols].astype(f32) + near(send[:, :cols], 2).astype(f32)
    other = near(keep[:, cols:], 4).astype(f32) + near(send[:, cols:], 6).astype(f32)
    both = jnp.stack(ordered(xlo, here, other))
    return (both + down_bias).astype(bf16)


def solution(mesh):
    fine = Mesh(mesh.devices.reshape(NY, NXLO, NXHI, NZ, NCORE), SEC + DEV)
    in_specs = (
        P(None, None, SEC + DEV),
        P(SEC),
        P(SEC),
        P(SEC, DEV),
        P(DEV),
        P(DEV, SEC),
        P(SEC),
    )
    return jax.shard_map(
        local, mesh=fine, in_specs=in_specs, out_specs=P(None, DEV, SEC), check_vma=False
    )
```

```python
import jax
import jax.numpy as jnp
from jax import lax
from jax.sharding import Mesh, PartitionSpec as P

f32, bf16 = jnp.float32, jnp.bfloat16
NY, NXLO, NXHI, NZ, NCORE = 4, 2, 2, 8, 2
SEC = ("y", "xlo")
DEV = ("xhi", "z", "core")
NEAR = ("xlo", "xhi", "core")


def swap(x, axis):
    return lax.ppermute(x, axis, [(0, 1), (1, 0)])


def turn(x, axis, d):
    n = lax.axis_size(axis)
    pairs = [(i * 2 + c, (i + d * (1 - 2 * c)) % n * 2 + c) for i in range(n) for c in range(2)]
    return lax.ppermute(x, (axis, "core"), pairs)


def near(x, mask):
    return lax.ppermute(x, NEAR, [(i, i ^ mask) for i in range(8)])


def flip(x, axis, bit):
    return lax.ppermute(x, axis, [(i, i ^ bit) for i in range(lax.axis_size(axis))])


def after(x, other):
    return lax.optimization_barrier((x, other))[0]


def ordered(which, own, other):
    first = which == 0
    return jnp.where(first, own, other), jnp.where(first, other, own)


def add(a, b):
    return (a.astype(f32) + b.astype(f32)).astype(bf16)


def ring_sum(down, z, way, other):
    rows, cols = down.shape[0] // NZ, down.shape[1]
    half = cols // 2

    def block(d):
        return lax.dynamic_slice_in_dim(down, (z + d * way + NZ) % NZ * rows, rows, 0)

    opposite = block(NZ // 2)
    there = turn(opposite[:, :half], "z", 1)
    back = turn(opposite[:, half:], "z", -1)
    for d in range(NZ // 2 - 1, 0, -1):
        a, b = block(d), block(-d)
        if d == 2:
            a, b = after((a, b), other)
        if d == NZ // 2 - 1:
            a = jnp.concatenate([add(a[:, :half], there), a[:, half:]], axis=1)
            b = jnp.concatenate([b[:, :half], add(b[:, half:], back)], axis=1)
        else:
            a, b = add(a, there), add(b, back)
        there, back = turn(a, "z", 1), turn(b, "z", -1)
    return block(0).astype(f32) + there.astype(f32) + back.astype(f32)


def local(acts, ln_gain, ln_bias, w1, up_bias, w2, down_bias):
    micros, seq, width = acts.shape
    own_seq = seq // (NXHI * NZ * NCORE)
    chunk = NZ * own_seq
    tokens = NXHI * chunk
    y, xlo, xhi, z, core = (lax.axis_index(a) for a in ("y", "xlo", "xhi", "z", "core"))
    features = width * 256
    way = 1 - 2 * core

    tiles = acts.reshape(micros, NXHI, NZ, NCORE, own_seq, width)
    tiles = tiles.transpose(0, 3, 5, 1, 2, 4).reshape(micros, NCORE, width, tokens)
    mine, theirs = ordered(xlo, tiles[0], tiles[1])
    quarter = [ordered(core, part[0], part[1]) for part in (mine, theirs)]

    def arrived(rx, rh, rc):
        piece, mask = quarter[rx][rc], rx * 4 + rh * 2 + rc
        return near(piece, mask) if mask else piece

    pieces = [[[arrived(rx, rh, rc) for rc in range(2)] for rh in range(2)] for rx in range(2)]
    rows = []
    for rx in range(2):
        by_hi = []
        for rh in range(2):
            a, b = ordered(core, *pieces[rx][rh])
            by_hi.append(jnp.concatenate([a, b], axis=0))
        rows.append(jnp.stack(ordered(xhi, *by_hi)))
    x = jnp.stack(rows)

    k1, n1 = w1.shape
    w1 = after(w1, pieces[0][0][1])
    scaled = (w1.astype(f32) * ln_gain[:, None]).astype(bf16)
    col = jnp.sum(scaled.astype(f32), axis=0)
    shifted = jnp.sum(w1.astype(f32) * ln_bias[:, None], axis=0)
    vec = jnp.stack([col, shifted])
    vec = vec + swap(vec, "xlo")
    x, scaled = lax.optimization_barrier((x, after(scaled, vec)))
    vecs = [vec, swap(vec, "core")]

    scaled = scaled.reshape(NXHI, NZ, 2 * width, n1).transpose(1, 0, 2, 3).reshape(k1, n1)
    far = swap(scaled, "xlo")
    scaled_other = swap(scaled, "core")

    spans = [(t * chunk, (t + 1) * chunk) for t in range(NXHI)]
    gathers = [lax.all_gather(x[..., i:j], "z") for i, j in spans]

    count = x.shape[0] * x.shape[1] * x.shape[2]
    x32 = x.astype(f32)
    mean = (jnp.sum(x32, axis=(0, 1, 2)) / count)[None]
    m2 = jnp.sum(jnp.square(x32 - mean), axis=(0, 1, 2))[None]
    mean = after(mean, (vecs[1], scaled_other))
    for axis, bit in (("y", 1), ("y", 2), ("z", 1), ("z", 2), ("z", 4)):
        theirs = flip(jnp.concatenate([mean, m2]), axis, bit)
        m2 = m2 + theirs[1:] + (count / 2) * jnp.square(mean - theirs[:1])
        mean, count = (mean + theirs[:1]) / 2, 2 * count
    mean, rstd = mean.reshape(-1, 1), lax.rsqrt(m2 / features + 1e-05).reshape(-1, 1)
    far = after(far, m2)
    far2 = swap(after(w2, far), "xlo")
    bias = jnp.concatenate([up_bias[None], swap(up_bias[None], "core")], axis=1)

    def project_up(t, j, xs, ws):
        cut = slice(*spans[t])
        acc = sum(
            lax.dot_general(g, w, (((0,), (0,)), ((), ())), preferred_element_type=f32)
            for g, w in zip(xs, ws)
        )
        return ((acc - mean[cut] * vecs[j][0]) * rstd[cut] + vecs[j][1]).astype(bf16)

    def by_section(gathered):
        return [gathered[:, r].reshape(k1, -1) for r in range(NXLO)]

    def spread(ups):
        part = ups[0].shape[0] // NY

        def block(d):
            at = (y + d + NY) % NY * part
            return jnp.concatenate(
                [lax.dynamic_slice_in_dim(up, at, part, 0) for up in ups], axis=1
            )

        return [block(0), turn(block(2), "y", 2)] + [
            turn(block(d * way), "y", d) for d in (1, -1)
        ]

    def activate(terms):
        total = sum(term.astype(f32) for term in terms)
        return jax.nn.gelu(total + bias, approximate=True).astype(bf16)

    def share(act):
        return [turn(act, "y", d) for d in (2, 1, -1)]

    def project_down(w2_cat, act, others):
        part = act.shape[0]
        hidden = jnp.zeros((NY * part, NCORE * n1), bf16)
        for d, got in zip((0, 2, -way, way), [act] + others):
            hidden = lax.dynamic_update_slice_in_dim(hidden, got, (y + d + NY) % NY * part, 0)
        return jnp.dot(hidden, w2_cat, preferred_element_type=f32).astype(bf16)

    xs0 = by_section(gathers[0])
    up0 = [project_up(0, 0, xs0, (scaled, far))]
    far_other = after(swap(far, "core"), up0[0])
    up0.append(project_up(0, 1, xs0, (scaled_other, far_other)))
    terms0 = spread(up0)
    act0 = activate(terms0)
    acts0 = share(act0)
    xs1 = by_section(after(gathers[1], act0))
    up1 = [project_up(1, 0, xs1, (scaled, far))]
    up1.append(project_up(1, 1, after(xs1, (up1[0], acts0[0])), (scaled_other, far_other)))
    terms1 = spread(up1)
    far2 = after(far2, act0)
    w2_cat = jnp.concatenate(
        [
            jnp.concatenate([w2, far2], axis=1),
            jnp.concatenate([swap(w2, "core"), swap(far2, "core")], axis=1),
        ],
        axis=0,
    )
    down0 = project_down(w2_cat, act0, after(acts0, up1))
    outs = [lax.psum_scatter(down0, "z", scatter_dimension=0, tiled=True)]
    act1 = activate(terms1[:1] + after(terms1[1:], down0))
    down1 = project_down(w2_cat, act1, share(act1))
    outs.append(ring_sum(down1, z, way, outs[0]).astype(bf16))

    keep, send = ordered(xhi, outs[0], outs[1])
    cols = down_bias.shape[0]
    here = keep[:, :cols].astype(f32) + near(send[:, :cols], 2).astype(f32)
    other = near(keep[:, cols:], 4).astype(f32) + near(send[:, cols:], 6).astype(f32)
    both = jnp.stack(ordered(xlo, here, other))
    return (both + down_bias).astype(bf16)


def solution(mesh):
    fine = Mesh(mesh.devices.reshape(NY, NXLO, NXHI, NZ, NCORE), SEC + DEV)
    in_specs = (
        P(None, None, SEC + DEV),
        P(SEC),
        P(SEC),
        P(SEC, DEV),
        P(DEV),
        P(DEV, SEC),
        P(SEC),
    )
    return jax.shard_map(
        local, mesh=fine, in_specs=in_specs, out_specs=P(None, DEV, SEC), check_vma=False
    )
```

```python
import jax
import jax.numpy as jnp
from jax import lax
from jax.sharding import Mesh, PartitionSpec as P

f32, bf16 = jnp.float32, jnp.bfloat16
NY, NXLO, NXHI, NZ, NCORE = 4, 2, 2, 8, 2
SEC = ("y", "xlo")
DEV = ("xhi", "z", "core")
NEAR = ("xlo", "xhi", "core")


def swap(x, axis):
    return lax.ppermute(x, axis, [(0, 1), (1, 0)])


def turn(x, axis, d):
    n = lax.axis_size(axis)
    pairs = [(i * 2 + c, (i + d * (1 - 2 * c)) % n * 2 + c) for i in range(n) for c in range(2)]
    return lax.ppermute(x, (axis, "core"), pairs)


def near(x, mask):
    return lax.ppermute(x, NEAR, [(i, i ^ mask) for i in range(8)])


def flip(x, axis, bit):
    return lax.ppermute(x, axis, [(i, i ^ bit) for i in range(lax.axis_size(axis))])


def after(x, other):
    return lax.optimization_barrier((x, other))[0]


def ordered(which, own, other):
    first = which == 0
    return jnp.where(first, own, other), jnp.where(first, other, own)


def add(a, b):
    return (a.astype(f32) + b.astype(f32)).astype(bf16)


def ring_sum(down, z, way, other):
    rows, cols = down.shape[0] // NZ, down.shape[1]
    half = cols // 2

    def block(d):
        return lax.dynamic_slice_in_dim(down, (z + d * way + NZ) % NZ * rows, rows, 0)

    opposite = block(NZ // 2)
    there = turn(opposite[:, :half], "z", 1)
    back = turn(opposite[:, half:], "z", -1)
    for d in range(NZ // 2 - 1, 0, -1):
        a, b = block(d), block(-d)
        if d == 3:
            a, b = after((a, b), other)
        if d == NZ // 2 - 1:
            a = jnp.concatenate([add(a[:, :half], there), a[:, half:]], axis=1)
            b = jnp.concatenate([b[:, :half], add(b[:, half:], back)], axis=1)
        else:
            a, b = add(a, there), add(b, back)
        there, back = turn(a, "z", 1), turn(b, "z", -1)
    return block(0).astype(f32) + there.astype(f32) + back.astype(f32)


def local(acts, ln_gain, ln_bias, w1, up_bias, w2, down_bias):
    micros, seq, width = acts.shape
    own_seq = seq // (NXHI * NZ * NCORE)
    chunk = NZ * own_seq
    tokens = NXHI * chunk
    y, xlo, xhi, z, core = (lax.axis_index(a) for a in ("y", "xlo", "xhi", "z", "core"))
    features = width * 256
    way = 1 - 2 * core

    tiles = acts.reshape(micros, NXHI, NZ, NCORE, own_seq, width)
    tiles = tiles.transpose(0, 3, 5, 1, 2, 4).reshape(micros, NCORE, width, tokens)
    mine, theirs = ordered(xlo, tiles[0], tiles[1])
    quarter = [ordered(core, part[0], part[1]) for part in (mine, theirs)]

    def arrived(rx, rh, rc):
        piece, mask = quarter[rx][rc], rx * 4 + rh * 2 + rc
        return near(piece, mask) if mask else piece

    pieces = [[[arrived(rx, rh, rc) for rc in range(2)] for rh in range(2)] for rx in range(2)]
    rows = []
    for rx in range(2):
        by_hi = []
        for rh in range(2):
            a, b = ordered(core, *pieces[rx][rh])
            by_hi.append(jnp.concatenate([a, b], axis=0))
        rows.append(jnp.stack(ordered(xhi, *by_hi)))
    x = jnp.stack(rows)

    k1, n1 = w1.shape
    w1 = after(w1, pieces[0][0][1])
    scaled = (w1.astype(f32) * ln_gain[:, None]).astype(bf16)
    col = jnp.sum(scaled.astype(f32), axis=0)
    shifted = jnp.sum(w1.astype(f32) * ln_bias[:, None], axis=0)
    vec = jnp.stack([col, shifted])
    vec = vec + swap(vec, "xlo")
    scaled = scaled.reshape(NXHI, NZ, 2 * width, n1).transpose(1, 0, 2, 3).reshape(k1, n1)
    x, scaled = lax.optimization_barrier((x, after(scaled, vec)))
    vecs = [vec, swap(vec, "core")]

    far = swap(scaled, "xlo")
    scaled_other = swap(scaled, "core")

    spans = [(t * chunk, (t + 1) * chunk) for t in range(NXHI)]
    gathers = [lax.all_gather(x[..., i:j], "z") for i, j in spans]

    count = x.shape[0] * x.shape[1] * x.shape[2]
    x32 = x.astype(f32)
    mean = (jnp.sum(x32, axis=(0, 1, 2)) / count)[None]
    m2 = jnp.sum(jnp.square(x32 - mean), axis=(0, 1, 2))[None]
    mean = after(mean, (vecs[1], scaled_other))
    for axis, bit in (("y", 1), ("y", 2), ("z", 1), ("z", 2), ("z", 4)):
        theirs = flip(jnp.concatenate([mean, m2]), axis, bit)
        m2 = m2 + theirs[1:] + (count / 2) * jnp.square(mean - theirs[:1])
        mean, count = (mean + theirs[:1]) / 2, 2 * count
    mean, rstd = mean.reshape(-1, 1), lax.rsqrt(m2 / features + 1e-05).reshape(-1, 1)
    far = after(far, m2)
    far2 = swap(after(w2, far), "xlo")
    bias = jnp.concatenate([up_bias[None], swap(up_bias[None], "core")], axis=1)

    def project_up(t, j, xs, ws):
        cut = slice(*spans[t])
        acc = sum(
            lax.dot_general(g, w, (((0,), (0,)), ((), ())), preferred_element_type=f32)
            for g, w in zip(xs, ws)
        )
        return ((acc - mean[cut] * vecs[j][0]) * rstd[cut] + vecs[j][1]).astype(bf16)

    def by_section(gathered):
        return [gathered[:, r].reshape(k1, -1) for r in range(NXLO)]

    def spread(ups):
        part = ups[0].shape[0] // NY

        def block(d):
            at = (y + d + NY) % NY * part
            return jnp.concatenate(
                [lax.dynamic_slice_in_dim(up, at, part, 0) for up in ups], axis=1
            )

        return [block(0), turn(block(2), "y", 2)] + [
            turn(block(d * way), "y", d) for d in (1, -1)
        ]

    def activate(terms):
        total = sum(term.astype(f32) for term in terms)
        return jax.nn.gelu(total + bias, approximate=True).astype(bf16)

    def share(act):
        return [turn(act, "y", d) for d in (2, 1, -1)]

    def project_down(w2_cat, act, others):
        part = act.shape[0]
        hidden = jnp.zeros((NY * part, NCORE * n1), bf16)
        for d, got in zip((0, 2, -way, way), [act] + others):
            hidden = lax.dynamic_update_slice_in_dim(hidden, got, (y + d + NY) % NY * part, 0)
        return jnp.dot(hidden, w2_cat, preferred_element_type=f32).astype(bf16)

    xs0 = by_section(gathers[0])
    up0 = [project_up(0, 0, xs0, (scaled, far))]
    far_other = after(swap(far, "core"), up0[0])
    up0.append(project_up(0, 1, xs0, (scaled_other, far_other)))
    terms0 = spread(up0)
    act0 = activate(terms0)
    acts0 = share(act0)
    xs1 = by_section(after(gathers[1], act0))
    up1 = [project_up(1, 0, xs1, (scaled, far))]
    up1.append(project_up(1, 1, after(xs1, (up1[0], acts0[0])), (scaled_other, far_other)))
    terms1 = spread(up1)
    far2 = after(far2, act0)
    w2_cat = jnp.concatenate(
        [
            jnp.concatenate([w2, far2], axis=1),
            jnp.concatenate([swap(w2, "core"), swap(far2, "core")], axis=1),
        ],
        axis=0,
    )
    down0 = project_down(w2_cat, after(act0, acts0[0]), after(acts0, up1))
    outs = [lax.psum_scatter(down0, "z", scatter_dimension=0, tiled=True)]
    act1 = activate(terms1[:1] + after(terms1[1:], down0))
    acts1 = share(act1)
    down1 = project_down(w2_cat, after(act1, acts1[0]), acts1)
    outs.append(ring_sum(down1, z, way, outs[0]).astype(bf16))

    keep, send = ordered(xhi, outs[0], outs[1])
    cols = down_bias.shape[0]
    here = keep[:, :cols].astype(f32) + near(send[:, :cols], 2).astype(f32)
    other = near(keep[:, cols:], 4).astype(f32) + near(send[:, cols:], 6).astype(f32)
    both = jnp.stack(ordered(xlo, here, other))
    return (both + down_bias).astype(bf16)


def solution(mesh):
    fine = Mesh(mesh.devices.reshape(NY, NXLO, NXHI, NZ, NCORE), SEC + DEV)
    in_specs = (
        P(None, None, SEC + DEV),
        P(SEC),
        P(SEC),
        P(SEC, DEV),
        P(DEV),
        P(DEV, SEC),
        P(SEC),
    )
    return jax.shard_map(
        local, mesh=fine, in_specs=in_specs, out_specs=P(None, DEV, SEC), check_vma=False
    )
```

```python
import jax
import jax.numpy as jnp
from jax import lax
from jax.sharding import Mesh, PartitionSpec as P

f32, bf16 = jnp.float32, jnp.bfloat16
NY, NXLO, NXHI, NZ, NCORE = 4, 2, 2, 8, 2
SEC = ("y", "xlo")
DEV = ("xhi", "z", "core")
NEAR = ("xlo", "xhi", "core")


def swap(x, axis):
    return lax.ppermute(x, axis, [(0, 1), (1, 0)])


def turn(x, axis, d):
    n = lax.axis_size(axis)
    pairs = [(i * 2 + c, (i + d * (1 - 2 * c)) % n * 2 + c) for i in range(n) for c in range(2)]
    return lax.ppermute(x, (axis, "core"), pairs)


def near(x, mask):
    return lax.ppermute(x, NEAR, [(i, i ^ mask) for i in range(8)])


def flip(x, axis, bit):
    return lax.ppermute(x, axis, [(i, i ^ bit) for i in range(lax.axis_size(axis))])


def after(x, other):
    return lax.optimization_barrier((x, other))[0]


def ordered(which, own, other):
    first = which == 0
    return jnp.where(first, own, other), jnp.where(first, other, own)


def add(a, b):
    return (a.astype(f32) + b.astype(f32)).astype(bf16)


def ring_sum(down, z, way, other):
    rows, cols = down.shape[0] // NZ, down.shape[1]
    half = cols // 2

    def block(d):
        return lax.dynamic_slice_in_dim(down, (z + d * way + NZ) % NZ * rows, rows, 0)

    opposite = block(NZ // 2)
    there = turn(opposite[:, :half], "z", 1)
    back = turn(opposite[:, half:], "z", -1)
    for d in range(NZ // 2 - 1, 0, -1):
        a, b = block(d), block(-d)
        if d == 3:
            a, b = after((a, b), other)
        if d == NZ // 2 - 1:
            a = jnp.concatenate([add(a[:, :half], there), a[:, half:]], axis=1)
            b = jnp.concatenate([b[:, :half], add(b[:, half:], back)], axis=1)
        else:
            a, b = add(a, there), add(b, back)
        there, back = turn(a, "z", 1), turn(b, "z", -1)
    return block(0).astype(f32) + there.astype(f32) + back.astype(f32)


def local(acts, ln_gain, ln_bias, w1, up_bias, w2, down_bias):
    micros, seq, width = acts.shape
    own_seq = seq // (NXHI * NZ * NCORE)
    chunk = NZ * own_seq
    tokens = NXHI * chunk
    y, xlo, xhi, z, core = (lax.axis_index(a) for a in ("y", "xlo", "xhi", "z", "core"))
    features = width * 256
    way = 1 - 2 * core

    tiles = acts.reshape(micros, NXHI, NZ, NCORE, own_seq, width)
    tiles = tiles.transpose(0, 3, 5, 1, 2, 4).reshape(micros, NCORE, width, tokens)
    mine, theirs = ordered(xlo, tiles[0], tiles[1])
    quarter = [ordered(core, part[0], part[1]) for part in (mine, theirs)]

    def arrived(rx, rh, rc):
        piece, mask = quarter[rx][rc], rx * 4 + rh * 2 + rc
        return near(piece, mask) if mask else piece

    pieces = [[[arrived(rx, rh, rc) for rc in range(2)] for rh in range(2)] for rx in range(2)]
    pieces[0][1][1], _ = lax.optimization_barrier((pieces[0][1][1], pieces[1][1][1]))
    rows = []
    for rx in range(2):
        by_hi = []
        for rh in range(2):
            a, b = ordered(core, *pieces[rx][rh])
            by_hi.append(jnp.concatenate([a, b], axis=0))
        rows.append(jnp.stack(ordered(xhi, *by_hi)))
    x = jnp.stack(rows)

    k1, n1 = w1.shape
    w1 = after(w1, pieces[0][0][1])
    scaled = (w1.astype(f32) * ln_gain[:, None]).astype(bf16)
    col = jnp.sum(scaled.astype(f32), axis=0)
    shifted = jnp.sum(w1.astype(f32) * ln_bias[:, None], axis=0)
    vec = jnp.stack([col, shifted])
    vec = vec + swap(vec, "xlo")
    scaled = scaled.reshape(NXHI, NZ, 2 * width, n1).transpose(1, 0, 2, 3).reshape(k1, n1)
    x, scaled = lax.optimization_barrier((x, after(scaled, vec)))
    vecs = [vec, swap(vec, "core")]

    far = swap(scaled, "xlo")
    scaled_other = swap(scaled, "core")

    spans = [(t * chunk, (t + 1) * chunk) for t in range(NXHI)]
    gathers = [lax.all_gather(x[..., i:j], "z") for i, j in spans]

    count = x.shape[0] * x.shape[1] * x.shape[2]
    x32 = x.astype(f32)
    mean = (jnp.sum(x32, axis=(0, 1, 2)) / count)[None]
    m2 = jnp.sum(jnp.square(x32 - mean), axis=(0, 1, 2))[None]
    mean = after(mean, (vecs[1], scaled_other))
    for axis, bit in (("y", 1), ("y", 2), ("z", 1), ("z", 2), ("z", 4)):
        theirs = flip(jnp.concatenate([mean, m2]), axis, bit)
        m2 = m2 + theirs[1:] + (count / 2) * jnp.square(mean - theirs[:1])
        mean, count = (mean + theirs[:1]) / 2, 2 * count
    mean, rstd = mean.reshape(-1, 1), lax.rsqrt(m2 / features + 1e-05).reshape(-1, 1)
    far = after(far, m2)
    far2 = swap(after(w2, far), "xlo")
    bias = jnp.concatenate([up_bias[None], swap(up_bias[None], "core")], axis=1)

    def project_up(t, j, xs, ws):
        cut = slice(*spans[t])
        acc = sum(
            lax.dot_general(g, w, (((0,), (0,)), ((), ())), preferred_element_type=f32)
            for g, w in zip(xs, ws)
        )
        return ((acc - mean[cut] * vecs[j][0]) * rstd[cut] + vecs[j][1]).astype(bf16)

    def by_section(gathered):
        return [gathered[:, r].reshape(k1, -1) for r in range(NXLO)]

    def spread(ups):
        part = ups[0].shape[0] // NY

        def block(d):
            at = (y + d + NY) % NY * part
            return jnp.concatenate(
                [lax.dynamic_slice_in_dim(up, at, part, 0) for up in ups], axis=1
            )

        return [block(0), turn(block(2), "y", 2)] + [
            turn(block(d * way), "y", d) for d in (1, -1)
        ]

    def activate(terms):
        total = sum(term.astype(f32) for term in terms)
        return jax.nn.gelu(total + bias, approximate=True).astype(bf16)

    def share(act):
        return [turn(act, "y", d) for d in (2, 1, -1)]

    def project_down(w2_cat, act, others):
        part = act.shape[0]
        hidden = jnp.zeros((NY * part, NCORE * n1), bf16)
        for d, got in zip((0, 2, -way, way), [act] + others):
            hidden = lax.dynamic_update_slice_in_dim(hidden, got, (y + d + NY) % NY * part, 0)
        return jnp.dot(hidden, w2_cat, preferred_element_type=f32).astype(bf16)

    xs0 = by_section(gathers[0])
    up0 = [project_up(0, 0, xs0, (scaled, far))]
    far_other = after(swap(far, "core"), up0[0])
    up0.append(project_up(0, 1, xs0, (scaled_other, far_other)))
    terms0 = spread(up0)
    act0 = activate(terms0)
    acts0 = share(act0)
    xs1 = by_section(after(gathers[1], act0))
    up1 = [project_up(1, 0, xs1, (scaled, far))]
    up1.append(project_up(1, 1, after(xs1, (up1[0], acts0[0])), (scaled_other, far_other)))
    terms1 = spread(up1)
    far2 = after(far2, up1[0])
    w2_cat = jnp.concatenate(
        [
            jnp.concatenate([w2, far2], axis=1),
            jnp.concatenate([swap(w2, "core"), swap(far2, "core")], axis=1),
        ],
        axis=0,
    )
    down0 = project_down(w2_cat, after(act0, acts0[0]), after(acts0, up1))
    outs = [lax.psum_scatter(down0, "z", scatter_dimension=0, tiled=True)]
    act1 = activate(terms1[:1] + after(terms1[1:], down0))
    acts1 = share(act1)
    down1 = project_down(w2_cat, after(act1, acts1[0]), acts1)
    outs.append(ring_sum(down1, z, way, outs[0]).astype(bf16))

    keep, send = ordered(xhi, outs[0], outs[1])
    cols = down_bias.shape[0]
    here = keep[:, :cols].astype(f32) + near(send[:, :cols], 2).astype(f32)
    other = near(keep[:, cols:], 4).astype(f32) + near(send[:, cols:], 6).astype(f32)
    both = jnp.stack(ordered(xlo, here, other))
    return (both + down_bias).astype(bf16)


def solution(mesh):
    fine = Mesh(mesh.devices.reshape(NY, NXLO, NXHI, NZ, NCORE), SEC + DEV)
    in_specs = (
        P(None, None, SEC + DEV),
        P(SEC),
        P(SEC),
        P(SEC, DEV),
        P(DEV),
        P(DEV, SEC),
        P(SEC),
    )
    return jax.shard_map(
        local, mesh=fine, in_specs=in_specs, out_specs=P(None, DEV, SEC), check_vma=False
    )
```

```python
import jax
import jax.numpy as jnp
from jax import lax
from jax.sharding import Mesh, PartitionSpec as P

f32, bf16 = jnp.float32, jnp.bfloat16
NY, NXLO, NXHI, NZ, NCORE = 4, 2, 2, 8, 2
SEC = ("y", "xlo")
DEV = ("xhi", "z", "core")
NEAR = ("xlo", "xhi", "core")


def swap(x, axis):
    return lax.ppermute(x, axis, [(0, 1), (1, 0)])


def turn(x, axis, d):
    n = lax.axis_size(axis)
    pairs = [(i * 2 + c, (i + d * (1 - 2 * c)) % n * 2 + c) for i in range(n) for c in range(2)]
    return lax.ppermute(x, (axis, "core"), pairs)


def near(x, mask):
    return lax.ppermute(x, NEAR, [(i, i ^ mask) for i in range(8)])


def flip(x, axis, bit):
    return lax.ppermute(x, axis, [(i, i ^ bit) for i in range(lax.axis_size(axis))])


def after(x, other):
    return lax.optimization_barrier((x, other))[0]


def ordered(which, own, other):
    first = which == 0
    return jnp.where(first, own, other), jnp.where(first, other, own)


def add(a, b):
    return (a.astype(f32) + b.astype(f32)).astype(bf16)


def ring_sum(down, z, way, other):
    rows, cols = down.shape[0] // NZ, down.shape[1]
    half = cols // 2

    def block(d):
        return lax.dynamic_slice_in_dim(down, (z + d * way + NZ) % NZ * rows, rows, 0)

    opposite = block(NZ // 2)
    there = turn(opposite[:, :half], "z", 1)
    back = turn(opposite[:, half:], "z", -1)
    for d in range(NZ // 2 - 1, 0, -1):
        a, b = block(d), block(-d)
        if d == 2:
            a, b = after((a, b), other)
        if d == NZ // 2 - 1:
            a = jnp.concatenate([add(a[:, :half], there), a[:, half:]], axis=1)
            b = jnp.concatenate([b[:, :half], add(b[:, half:], back)], axis=1)
        else:
            a, b = add(a, there), add(b, back)
        there, back = turn(a, "z", 1), turn(b, "z", -1)
    return block(0).astype(f32) + there.astype(f32) + back.astype(f32)


def local(acts, ln_gain, ln_bias, w1, up_bias, w2, down_bias):
    micros, seq, width = acts.shape
    own_seq = seq // (NXHI * NZ * NCORE)
    chunk = NZ * own_seq
    tokens = NXHI * chunk
    y, xlo, xhi, z, core = (lax.axis_index(a) for a in ("y", "xlo", "xhi", "z", "core"))
    features = width * 256
    way = 1 - 2 * core

    tiles = acts.reshape(micros, NXHI, NZ, NCORE, own_seq, width)
    tiles = tiles.transpose(0, 3, 5, 1, 2, 4).reshape(micros, NCORE, width, tokens)
    mine, theirs = ordered(xlo, tiles[0], tiles[1])
    quarter = [ordered(core, part[0], part[1]) for part in (mine, theirs)]

    def arrived(rx, rh, rc):
        piece, mask = quarter[rx][rc], rx * 4 + rh * 2 + rc
        return near(piece, mask) if mask else piece

    pieces = [[[arrived(rx, rh, rc) for rc in range(2)] for rh in range(2)] for rx in range(2)]
    pieces[0][1][1], _ = lax.optimization_barrier((pieces[0][1][1], pieces[1][1][1]))
    rows = []
    for rx in range(2):
        by_hi = []
        for rh in range(2):
            a, b = ordered(core, *pieces[rx][rh])
            by_hi.append(jnp.concatenate([a, b], axis=0))
        rows.append(jnp.stack(ordered(xhi, *by_hi)))
    x = jnp.stack(rows)

    k1, n1 = w1.shape
    w1 = after(w1, pieces[0][0][1])
    scaled = (w1.astype(f32) * ln_gain[:, None]).astype(bf16)
    col = jnp.sum(scaled.astype(f32), axis=0)
    shifted = jnp.sum(w1.astype(f32) * ln_bias[:, None], axis=0)
    vec = jnp.stack([col, shifted])
    vec = vec + swap(vec, "xlo")
    scaled = scaled.reshape(NXHI, NZ, 2 * width, n1).transpose(1, 0, 2, 3).reshape(k1, n1)
    x, scaled = lax.optimization_barrier((x, after(scaled, vec)))
    vecs = [vec, swap(vec, "core")]

    far = swap(scaled, "xlo")
    scaled_other = swap(scaled, "core")

    spans = [(t * chunk, (t + 1) * chunk) for t in range(NXHI)]
    gathers = [lax.all_gather(x[..., i:j], "z") for i, j in spans]

    count = x.shape[0] * x.shape[1] * x.shape[2]
    x32 = x.astype(f32)
    mean = (jnp.sum(x32, axis=(0, 1, 2)) / count)[None]
    m2 = jnp.sum(jnp.square(x32 - mean), axis=(0, 1, 2))[None]
    mean = after(mean, (vecs[1], scaled_other))
    for axis, bit in (("y", 1), ("y", 2), ("z", 1), ("z", 2), ("z", 4)):
        theirs = flip(jnp.concatenate([mean, m2]), axis, bit)
        m2 = m2 + theirs[1:] + (count / 2) * jnp.square(mean - theirs[:1])
        mean, count = (mean + theirs[:1]) / 2, 2 * count
    mean, rstd = mean.reshape(-1, 1), lax.rsqrt(m2 / features + 1e-05).reshape(-1, 1)
    far = after(far, m2)
    far2 = swap(after(w2, far), "xlo")
    bias = jnp.concatenate([up_bias[None], swap(up_bias[None], "core")], axis=1)

    def project_up(t, j, xs, ws):
        cut = slice(*spans[t])
        acc = sum(
            lax.dot_general(g, w, (((0,), (0,)), ((), ())), preferred_element_type=f32)
            for g, w in zip(xs, ws)
        )
        return ((acc - mean[cut] * vecs[j][0]) * rstd[cut] + vecs[j][1]).astype(bf16)

    def by_section(gathered):
        return [gathered[:, r].reshape(k1, -1) for r in range(NXLO)]

    def spread(ups):
        part = ups[0].shape[0] // NY

        def block(d):
            at = (y + d + NY) % NY * part
            return jnp.concatenate(
                [lax.dynamic_slice_in_dim(up, at, part, 0) for up in ups], axis=1
            )

        return [block(0), turn(block(2), "y", 2)] + [
            turn(block(d * way), "y", d) for d in (1, -1)
        ]

    def activate(terms):
        total = sum(term.astype(f32) for term in terms)
        return jax.nn.gelu(total + bias, approximate=True).astype(bf16)

    def share(act):
        return [turn(act, "y", d) for d in (2, 1, -1)]

    def project_down(w2_cat, act, others):
        part = act.shape[0]
        hidden = jnp.zeros((NY * part, NCORE * n1), bf16)
        for d, got in zip((0, 2, -way, way), [act] + others):
            hidden = lax.dynamic_update_slice_in_dim(hidden, got, (y + d + NY) % NY * part, 0)
        return jnp.dot(hidden, w2_cat, preferred_element_type=f32).astype(bf16)

    xs0 = by_section(gathers[0])
    up0 = [project_up(0, 0, xs0, (scaled, far))]
    far_other = after(swap(far, "core"), up0[0])
    up0.append(project_up(0, 1, xs0, (scaled_other, far_other)))
    terms0 = spread(up0)
    act0 = activate(terms0)
    acts0 = share(act0)
    xs1 = by_section(after(gathers[1], act0))
    up1 = [project_up(1, 0, xs1, (scaled, far))]
    up1.append(project_up(1, 1, after(xs1, (up1[0], acts0[0])), (scaled_other, far_other)))
    terms1 = spread(up1)
    far2 = after(far2, up1[0])
    w2_cat = jnp.concatenate(
        [
            jnp.concatenate([w2, far2], axis=1),
            jnp.concatenate([swap(w2, "core"), swap(far2, "core")], axis=1),
        ],
        axis=0,
    )
    down0 = project_down(w2_cat, after(act0, acts0[0]), after(acts0, up1))
    outs = [lax.psum_scatter(down0, "z", scatter_dimension=0, tiled=True)]
    act1 = activate(terms1[:1] + after(terms1[1:], down0))
    down1 = project_down(w2_cat, act1, share(act1))
    outs.append(ring_sum(down1, z, way, outs[0]).astype(bf16))

    keep, send = ordered(xhi, outs[0], outs[1])
    cols = down_bias.shape[0]
    here = keep[:, :cols].astype(f32) + near(send[:, :cols], 2).astype(f32)
    other = near(keep[:, cols:], 4).astype(f32) + near(send[:, cols:], 6).astype(f32)
    both = jnp.stack(ordered(xlo, here, other))
    return (both + down_bias).astype(bf16)


def solution(mesh):
    fine = Mesh(mesh.devices.reshape(NY, NXLO, NXHI, NZ, NCORE), SEC + DEV)
    in_specs = (
        P(None, None, SEC + DEV),
        P(SEC),
        P(SEC),
        P(SEC, DEV),
        P(DEV),
        P(DEV, SEC),
        P(SEC),
    )
    return jax.shard_map(
        local, mesh=fine, in_specs=in_specs, out_specs=P(None, DEV, SEC), check_vma=False
    )
```
